128 devices in a mesh: head: 4 (over y), probe: 32 (over z, x, core).
Axes of the slice: x: 4, y: 4, z: 4, core: 2. Of those that a mesh axis runs over, the one named last changes fastest.
Arguments:
- history_keys: bfloat16 [8, 16384, 128], P('head'), may hold values from -4 to 4, as said below
- history_values: bfloat16 [8, 16384, 128], P('head'), as said below
- queries: bfloat16 [8, 16384, 128], P('head', 'probe'), as said below
- positions: int32 [8, 16384], P('head', 'probe'), may hold values from 8192 to 16383
- kept_index: int32 [8, 2048], P('head'), may hold values from 0 to 16383, as said below
Outputs:
- correction: float32 [8, 2048, 128], P('head', 'probe')
The draws below stay inside these ranges and needn't reach their ends.
Inputs may be any that keep to these rules, and one draw needn't show every extreme that they name: `kept_index`: in each head, slot i holds a history position in [i * 8, (i + 1) * 8); slot 0 holds position 0 and the last slot position 16383. `queries`: probe query vectors of each head. `history_keys`: history keys of each head. `history_values`: history values of each head.
All inputs are finite; a program needn't handle non-finite values.
Results may differ from the reference program's by a relative error of at most 0.0006.
Values sent between devices are 32-bit elements; how exact they have to be, the bound alone decides.
No kernel may reach another device: no remote copies, remote signals or barrier semaphores. Data moves between devices by JAX's collectives and lax.ppermute only.
A program may use at most 128 MiB of HBM per device.

```python
import math
import jax
import jax.numpy as jnp
from jax import lax

KV = 8
HD = 128
HIST = 16384
KEPT = 2048
ITERS = 2
PROBES = 16384


def kept_slots(key):
    stride = HIST // KEPT
    offsets = jax.random.randint(jax.random.fold_in(key, 101), (KV, KEPT), 0, stride)
    offsets = offsets.at[:, 0].set(0).at[:, KEPT - 1].set(stride - 1)
    return (jnp.arange(KEPT, dtype=jnp.int32)[None, :] * stride + offsets).astype(jnp.int32)


def drawn_keys(key):
    return jnp.clip(jax.random.normal(jax.random.fold_in(key, 102), (KV, HIST, HD), jnp.float32), -4.0, 4.0)


def draw_kept_index(key, part):
    return kept_slots(key)


def draw_history_keys(key, part):
    base = drawn_keys(key)
    return base.astype(jnp.bfloat16)


def draw_queries(key, part):
    own = jax.random.fold_in(key, 2)
    rows_all = 2.0 * jnp.clip(jax.random.normal(own, (KV, PROBES, HD), jnp.float32), -4.0, 4.0)
    return rows_all.astype(jnp.bfloat16)


def draw_history_values(key, part):
    own = jax.random.fold_in(key, 3)
    noise_key, row_key = jax.random.split(own)
    row_scale = 0.3 * jnp.exp(jax.random.uniform(row_key, (KV, HIST, 1), jnp.float32, 0.0, math.log(10.0)))
    ramp = jnp.arange(KV, dtype=jnp.float32) / (KV - 1)
    noise = jnp.clip(jax.random.normal(noise_key, (KV, HIST, HD), jnp.float32), -4.0, 4.0)
    head_scale = jnp.exp(math.log(3.0) * ramp)
    return (noise * row_scale * head_scale[:, None, None]).astype(jnp.bfloat16)


def touch_ends(entries, stream_key, low, largest):
    shape = entries.shape
    place = [jax.random.randint(jax.random.fold_in(stream_key, axis), (), 0, shape[axis]) for axis in range(len(shape))]
    entries = entries.at[tuple(place)].set(low)
    longest = shape.index(max(shape))
    place[longest] = (place[longest] + 1) % shape[longest]
    return entries.at[tuple(place)].set(largest)


def setup_inputs(seed: int = 0) -> dict:
    arg_keys = jax.random.split(jax.random.key(seed), 6)
    return {
        "history_keys": draw_history_keys(jax.random.fold_in(arg_keys[5], 71), 0),
        "history_values": draw_history_values(jax.random.fold_in(arg_keys[5], 71), 0),
        "queries": draw_queries(jax.random.fold_in(arg_keys[5], 71), 0),
        "positions": touch_ends(jax.random.randint(arg_keys[3], (KV, PROBES), HIST // 2, HIST), jax.random.fold_in(arg_keys[3], 1), HIST // 2, HIST - 1).astype(jnp.int32),
        "kept_index": draw_kept_index(jax.random.fold_in(arg_keys[5], 71), 0),
    }


HIGH = lax.Precision.HIGHEST

def masked_parts(scores, visible):
    peak = lax.optimization_barrier(jnp.max(jnp.where(visible, scores, -jnp.inf), axis=-1, keepdims=True))
    expo = jnp.exp(jnp.where(visible, scores - peak, -jnp.inf))
    return (expo, lax.optimization_barrier(jnp.sum(expo, axis=-1, keepdims=True)))

def head_target(keys, values, probe_rows, probe_pos):
    block = min(512, probe_rows.shape[0])
    scale = 1.0 / math.sqrt(probe_rows.shape[1])
    rows_blocks = probe_rows.reshape(-1, block, probe_rows.shape[1])
    pos_blocks = probe_pos.reshape(-1, block)
    order = jnp.arange(keys.shape[0], dtype=jnp.int32)

    def one_block(pieces):
        rows_now, pos_now = pieces
        scores = jnp.dot(rows_now, keys.T, preferred_element_type=jnp.float32) * scale
        visible = order[None, :] <= pos_now[:, None]
        expo, total = masked_parts(scores, visible)
        mixed = jnp.dot(expo.astype(jnp.bfloat16), values, preferred_element_type=jnp.float32)
        return mixed / total
    return lax.map(one_block, (rows_blocks, pos_blocks)).reshape(probe_rows.shape[0], -1)

def head_weights(kept_keys, kept_pos, probe_rows, probe_pos):
    scale = 1.0 / math.sqrt(probe_rows.shape[1])
    scores = jnp.dot(probe_rows, kept_keys.T, preferred_element_type=jnp.float32) * scale
    visible = kept_pos[None, :] <= probe_pos[:, None]
    expo, total = masked_parts(scores, visible)
    return expo / total

def reference(history_keys, history_values, queries, positions, kept_index):
    targets = lax.map(lambda pieces: head_target(*pieces), (history_keys, history_values, queries, positions))
    kept_keys = jnp.take_along_axis(history_keys, kept_index[:, :, None].astype(jnp.int32), axis=1)
    start_values = jnp.take_along_axis(history_values, kept_index[:, :, None].astype(jnp.int32), axis=1).astype(jnp.float32)
    ridge = PROBES / (KEPT * KEPT)

    def first_side(pieces):
        keys_now, kept_now, rows_now, pos_now, target_now, start_now = pieces
        weights = head_weights(keys_now, kept_now, rows_now, pos_now)
        gap = target_now - jnp.dot(weights, start_now, precision=HIGH, preferred_element_type=jnp.float32)
        return jnp.dot(weights.T, gap, precision=HIGH, preferred_element_type=jnp.float32)

    def normal_of(pieces):
        keys_now, kept_now, rows_now, pos_now, vec_now = pieces
        weights = head_weights(keys_now, kept_now, rows_now, pos_now)
        image = jnp.dot(weights, vec_now, precision=HIGH, preferred_element_type=jnp.float32)
        return jnp.dot(weights.T, image, precision=HIGH, preferred_element_type=jnp.float32) + ridge * vec_now
    residual = lax.map(first_side, (kept_keys, kept_index, queries, positions, targets, start_values))
    direction = residual
    norm_now = jnp.sum(residual * residual)
    correction = jnp.zeros_like(residual)
    for step in range(ITERS):
        image = lax.map(normal_of, (kept_keys, kept_index, queries, positions, direction))
        alpha = norm_now / jnp.sum(direction * image)
        correction = correction + alpha * direction
        if step + 1 < ITERS:
            residual = residual - alpha * image
            norm_next = jnp.sum(residual * residual)
            direction = residual + norm_next / norm_now * direction
            norm_now = norm_next
    return correction
```

```python
import functools
import math

import jax
import jax.numpy as jnp
from jax import lax
from jax.experimental import pallas as pl
from jax.experimental.pallas import tpu as pltpu
from jax.sharding import PartitionSpec as P

HD = 128
BLOCK = 2048
ROWS = 256
MIB = 1024 * 1024
f32 = jnp.float32
bf16 = jnp.bfloat16
NT = (((1,), (1,)), ((), ()))
NN = (((1,), (0,)), ((), ()))


def dot(left, right, dims=NN):
    return lax.dot_general(left, right, dims, preferred_element_type=f32)


def halves(wide):
    high = wide.astype(bf16)
    return high, (wide - high.astype(f32)).astype(bf16)


def column(ref, tile):
    return jnp.transpose(ref[...])[:, tile : tile + 1]


def attend_kernel(core, q_ref, pos_ref, kept_ref, k_ref, v_ref, t_ref, q2_ref, kk_ref, kv_ref, m_ref, acc_ref, k2_ref, v2_ref):
    step = pl.program_id(0)
    rows = q_ref.shape[0]
    tiles = rows // ROWS
    per = BLOCK // 8

    @pl.when(step == 0)
    def _():
        high, low = halves(q_ref[...])
        q2_ref[:, :HD] = high
        q2_ref[:, HD:] = low
        m_ref[...] = jnp.full(m_ref.shape, -jnp.inf, f32)
        acc_ref[...] = jnp.zeros(acc_ref.shape, f32)
        v2_ref[:, HD:] = jnp.ones((BLOCK, HD), bf16)

    keys = k_ref[0]
    values = v_ref[0]
    k2_ref[:, :HD] = keys
    k2_ref[:, HD:] = keys
    v2_ref[:, :HD] = values

    part = 1024
    slots = part // 8
    kept_cols = jnp.transpose(kept_ref[...])
    for piece in range(BLOCK // part):
        lane = lax.broadcasted_iota(jnp.int32, (slots, part), 1)
        want = kept_cols[:, piece : piece + 1] - (step * BLOCK + piece * part)
        hot = jnp.where(lane == want, 1.0, 0.0).astype(bf16)
        both = jnp.concatenate([k_ref[0, pl.ds(piece * part, part), :], v_ref[0, pl.ds(piece * part, part), :]], axis=1)
        got = dot(hot, both)
        kk_ref[pl.ds(piece * slots, slots), :] = got[:, :HD].astype(bf16)
        kv_ref[pl.ds(piece * slots, slots), :] = got[:, HD:].astype(bf16)

    def go(masked):
        pos_cols = jnp.transpose(pos_ref[...]).astype(jnp.int32) - step * BLOCK
        for tile in range(tiles):
            here = pl.ds(tile * ROWS, ROWS)
            scores = dot(q2_ref[here, :], k2_ref[...], NT)
            if masked:
                pos = jnp.concatenate(
                    [pos_cols[:, i : i + 1] for i in range(tile * ROWS // 128, (tile + 1) * ROWS // 128)], axis=0
                )
                lane = lax.broadcasted_iota(jnp.int32, scores.shape, 1)
                scores = jnp.where(lane <= pos, scores, -jnp.inf)
            old = m_ref[here, :]
            new = jnp.maximum(old, jnp.max(scores, axis=1, keepdims=True))
            m_ref[here, :] = new
            expo = jnp.exp2(scores - new[:, :1]).astype(bf16)
            fade = jnp.exp2(old - new)
            fade2 = jnp.concatenate([fade, fade], axis=1)
            acc_ref[here, :] = acc_ref[here, :] * fade2 + dot(expo, v2_ref[...])

    half = pl.num_programs(0) // 2

    @pl.when(step < half)
    def _():
        go(False)

    @pl.when(step >= half)
    def _():
        go(True)

    @pl.when(step == pl.num_programs(0) - 1)
    def _():
        t_ref[...] = acc_ref[:, :HD] / acc_ref[:, HD:]


def attend(core, q, pos, kept, keys, values):
    rows = q.shape[0]
    hist = keys.shape[1]
    steps = hist // BLOCK
    per = BLOCK // 8
    kept_count = kept.shape[0] * kept.shape[1]
    whole = lambda shape: pl.BlockSpec(shape, lambda j, c: (0,) * len(shape))
    return pl.pallas_call(
        attend_kernel,
        grid_spec=pltpu.PrefetchScalarGridSpec(
            num_scalar_prefetch=1,
            grid=(steps,),
            in_specs=[
                whole((rows, HD)),
                whole(pos.shape),
                pl.BlockSpec((None, per // 128, 128), lambda j, c: (j, 0, 0)),
                pl.BlockSpec((1, BLOCK, HD), lambda j, c: (c[0], j, 0)),
                pl.BlockSpec((1, BLOCK, HD), lambda j, c: (c[0], j, 0)),
            ],
            out_specs=[
                whole((rows, HD)),
                whole((rows, 2 * HD)),
                pl.BlockSpec((per, HD), lambda j, c: (j, 0)),
                pl.BlockSpec((per, HD), lambda j, c: (j, 0)),
            ],
            scratch_shapes=[
                pltpu.VMEM((rows, HD), f32),
                pltpu.VMEM((rows, 2 * HD), f32),
                pltpu.VMEM((BLOCK, 2 * HD), bf16),
                pltpu.VMEM((BLOCK, 2 * HD), bf16),
            ],
        ),
        out_shape=[
            jax.ShapeDtypeStruct((rows, HD), f32),
            jax.ShapeDtypeStruct((rows, 2 * HD), bf16),
            jax.ShapeDtypeStruct((kept_count, HD), bf16),
            jax.ShapeDtypeStruct((kept_count, HD), bf16),
        ],
        compiler_params=pltpu.CompilerParams(vmem_limit_bytes=40 * MIB),
        name="attend",
    )(core, q, pos, kept.reshape(steps, per // 128, 128), keys, values)


def pull_back(gap_t, wh, wl, z_ref, first):
    high, low = halves(gap_t)
    two = dot(jnp.concatenate([high, low], axis=0), wh)
    part = two[:HD] + two[HD:] + dot(high, wl)
    for chunk in range(z_ref.shape[0]):
        cut = part[:, chunk * 128 : (chunk + 1) * 128]

        @pl.when(first)
        def _():
            z_ref[chunk] = cut

        @pl.when(jnp.logical_not(first))
        def _():
            z_ref[chunk] += cut


def start_kernel(q2_ref, pos_ref, kept_ref, kk_ref, kv_ref, t_ref, wh_ref, wl_ref, z_ref, k2_ref):
    tile = pl.program_id(0)

    @pl.when(tile == 0)
    def _():
        k2_ref[:, :HD] = kk_ref[...]
        k2_ref[:, HD:] = kk_ref[...]

    scores = dot(q2_ref[...], k2_ref[...], NT)
    pos_cols = jnp.transpose(pos_ref[...]).astype(jnp.int32)
    pos = jnp.concatenate([pos_cols[:, i : i + 1] for i in range(ROWS // 128)], axis=0)
    scores = jnp.where(kept_ref[...] <= pos, scores, -jnp.inf)
    expo = jnp.exp2(scores - jnp.max(scores, axis=1, keepdims=True))
    weights = expo * (1.0 / jnp.sum(expo, axis=1, keepdims=True))
    wh, wl = halves(weights)
    wh_ref[...] = wh
    wl_ref[...] = wl
    gap = t_ref[...] - (dot(wh, kv_ref[...]) + dot(wl, kv_ref[...]))
    pull_back(jnp.transpose(gap), wh, wl, z_ref, tile == 0)


def start(q2, pos, kept, kept_keys, kept_values, target):
    rows = q2.shape[0]
    count = kept_keys.shape[0]
    whole = lambda shape: pl.BlockSpec(shape, lambda i: (0,) * len(shape))
    return pl.pallas_call(
        start_kernel,
        grid=(rows // ROWS,),
        in_specs=[
            pl.BlockSpec((ROWS, 2 * HD), lambda i: (i, 0)),
            pl.BlockSpec((None, ROWS // 128, 128), lambda i: (i, 0, 0)),
            whole((1, count)),
            whole((count, HD)),
            whole((count, HD)),
            pl.BlockSpec((ROWS, HD), lambda i: (i, 0)),
        ],
        out_specs=[
            pl.BlockSpec((ROWS, count), lambda i: (i, 0)),
            pl.BlockSpec((ROWS, count), lambda i: (i, 0)),
            whole((count // 128, HD, 128)),
        ],
        out_shape=[
            jax.ShapeDtypeStruct((rows, count), bf16),
            jax.ShapeDtypeStruct((rows, count), bf16),
            jax.ShapeDtypeStruct((count // 128, HD, 128), f32),
        ],
        scratch_shapes=[pltpu.VMEM((count, 2 * HD), bf16)],
        compiler_params=pltpu.CompilerParams(vmem_limit_bytes=40 * MIB),
        name="start",
    )(q2, pos.reshape(rows // ROWS, ROWS // 128, 128), kept.reshape(1, count), kept_keys, kept_values, target)


def load_vector(vec_ref, two_ref):
    for chunk in range(vec_ref.shape[0]):
        high, low = halves(vec_ref[chunk])
        two_ref[:HD, pl.ds(chunk * 128, 128)] = high
        two_ref[HD:, pl.ds(chunk * 128, 128)] = low


def push(two_ref, wh, wl):
    two = dot(two_ref[...], wh, NT)
    return two[:HD] + two[HD:] + dot(two_ref[:HD, :], wl, NT)


def normal_kernel(vec_ref, wh_ref, wl_ref, z_ref, two_ref):
    tile = pl.program_id(0)

    @pl.when(tile == 0)
    def _():
        load_vector(vec_ref, two_ref)

    wh = wh_ref[...]
    wl = wl_ref[...]
    pull_back(push(two_ref, wh, wl), wh, wl, z_ref, tile == 0)


def square_kernel(vec_ref, wh_ref, wl_ref, s_ref, two_ref):
    tile = pl.program_id(0)

    @pl.when(tile == 0)
    def _():
        load_vector(vec_ref, two_ref)
        s_ref[...] = jnp.zeros(s_ref.shape, f32)

    image = push(two_ref, wh_ref[...], wl_ref[...])
    s_ref[...] += jnp.sum(image * image, axis=0, keepdims=True)


def with_weights(kernel, name, out, vec, wh, wl):
    rows, count = wh.shape
    whole = lambda shape: pl.BlockSpec(shape, lambda i: (0,) * len(shape))
    return pl.pallas_call(
        kernel,
        grid=(rows // ROWS,),
        in_specs=[
            whole(vec.shape),
            pl.BlockSpec((ROWS, count), lambda i: (i, 0)),
            pl.BlockSpec((ROWS, count), lambda i: (i, 0)),
        ],
        out_specs=whole(out),
        out_shape=jax.ShapeDtypeStruct(out, f32),
        scratch_shapes=[pltpu.VMEM((2 * HD, count), bf16)],
        compiler_params=pltpu.CompilerParams(vmem_limit_bytes=40 * MIB),
        name=name,
    )(vec, wh, wl)


def local(history_keys, history_values, queries, positions, kept_index):
    count = kept_index.shape[1]
    own_rows = queries.shape[1]
    devices = lax.axis_size("probe")
    chips = devices // 2
    heads = lax.axis_size("head")
    ridge = own_rows * devices / (count * count)
    core = lax.rem(lax.axis_index("probe"), 2)
    swap = [(i, i ^ 1) for i in range(devices)]
    groups = [[2 * i + c for i in range(chips)] for c in range(2)]

    scaled = queries.astype(f32) * (math.log2(math.e) / math.sqrt(HD))
    packed = jnp.concatenate([scaled, positions.astype(f32).reshape(2, own_rows // 128, 128)], axis=1)
    mine = lax.dynamic_index_in_dim(packed, core, 0, keepdims=False)
    other = lax.ppermute(lax.dynamic_index_in_dim(packed, 1 - core, 0, keepdims=False), "probe", swap)
    q = jnp.concatenate([mine[:own_rows], other[:own_rows]], axis=0)
    pos = jnp.concatenate([mine[own_rows:], other[own_rows:]], axis=0)
    kept = lax.dynamic_index_in_dim(kept_index, core, 0, keepdims=False)

    target, q2, kept_keys, kept_values = attend(
        core.astype(jnp.int32).reshape(1), q, pos, kept.reshape(-1, 128), history_keys, history_values
    )
    wh, wl, z = start(q2, pos, kept, kept_keys, kept_values, target)

    def exchange(chunks):
        return lax.all_to_all(chunks, "probe", 0, 0, axis_index_groups=groups, tiled=True)

    def spread(chunk):
        return exchange(jnp.broadcast_to(chunk[None], (chips,) + chunk.shape))

    res = jnp.sum(exchange(z), axis=0)
    z = with_weights(normal_kernel, "normal", z.shape, spread(res), wh, wl)
    image = jnp.sum(exchange(z), axis=0) + ridge * res

    basis = jnp.transpose(jnp.stack([res, image]), (0, 2, 1))
    half = basis.shape[1] // 2
    kept_half = lax.dynamic_slice_in_dim(basis, core * half, half, 1)
    sent_half = lax.dynamic_slice_in_dim(basis, (1 - core) * half, half, 1)
    got_half = lax.ppermute(sent_half, "probe", swap)
    first = jnp.where(core == 0, kept_half, got_half)
    second = jnp.where(core == 0, got_half, kept_half)

    squares = with_weights(square_kernel, "square", (1, ROWS), spread(image), wh, wl)
    sums = jnp.stack([jnp.sum(res * res), jnp.sum(res * image), jnp.sum(image * image), jnp.sum(squares)])
    sums = jnp.broadcast_to(jnp.pad(sums, (0, 124))[None, None], (heads * devices, 1, 128))
    sums = jnp.sum(lax.all_to_all(sums, ("head", "probe"), 0, 0, tiled=True), axis=(0, 1))
    rr, rn, nn, ww = sums[0], sums[1], sums[2], sums[3]
    alpha = rr / rn
    new = rr - 2.0 * alpha * rn + alpha * alpha * nn
    beta = new / rr
    grow = 1.0 + beta
    curve = grow * grow * rn - 2.0 * alpha * grow * nn + alpha * alpha * (ww + ridge * nn)
    step = new / curve
    left = alpha + step * grow
    right = -step * alpha
    return jnp.stack([left * first[0] + right * first[1], left * second[0] + right * second[1]])


def solution(mesh):
    return jax.shard_map(
        local,
        mesh=mesh,
        in_specs=(
            P("head", None, None),
            P("head", None, None),
            P("head", "probe", None),
            P("head", "probe"),
            P("head", None),
        ),
        out_specs=P("head", "probe", None),
        check_vma=False,
    )
```

```python
import math

import jax
import jax.numpy as jnp
from jax import lax
from jax.experimental import pallas as pl
from jax.experimental.pallas import tpu as pltpu
from jax.sharding import PartitionSpec as P

HD = 128
LANES = 128
BLOCK = 2048
ROWS = 256
PICK = 256
LIMIT = 2.0**40
MIB = 1024 * 1024
f32 = jnp.float32
bf16 = jnp.bfloat16
NT = (((1,), (1,)), ((), ()))
NN = (((1,), (0,)), ((), ()))


def dot(left, right, dims=NN):
    return lax.dot_general(left, right, dims, preferred_element_type=f32)


def halves(wide):
    high = wide.astype(bf16)
    return high, (wide - high.astype(f32)).astype(bf16)


def stacked(wide):
    return jnp.concatenate(halves(wide), axis=0)


def whole(shape):
    return pl.BlockSpec(shape, lambda *ids: (0,) * len(shape))


def params():
    return pltpu.CompilerParams(vmem_limit_bytes=56 * MIB)


def columns_of(rows):
    return jnp.transpose(rows).astype(jnp.int32)


def stack_columns(cols, first, count):
    return jnp.concatenate([cols[:, i : i + 1] for i in range(first, first + count)], axis=0)


def attend_kernel(core, mine_ref, other_ref, kept_ref, k_ref, v_ref, k_any, v_any, t_ref, q2_ref, pos_ref, kk_ref, kv_ref, m_ref, acc_ref, k2_ref, v2_ref, sem):
    step = pl.program_id(0)
    steps = pl.num_programs(0)
    rows = q2_ref.shape[0]
    own = rows // 2
    tiles = rows // ROWS
    slots = PICK // 8

    @pl.when(step == 0)
    def _():
        for part, ref in enumerate((mine_ref.at[0], other_ref)):
            high, low = halves(ref[:own, :])
            q2_ref[pl.ds(part * own, own), :HD] = high
            q2_ref[pl.ds(part * own, own), HD:] = low
            pos_ref[pl.ds(part * own // LANES, own // LANES), :] = ref[own:, :]
        acc_ref[...] = jnp.zeros(acc_ref.shape, f32)
        v2_ref[:, HD:] = jnp.ones((BLOCK, HD), bf16)

    def load(keys, values):
        k2_ref[:, :HD] = keys
        k2_ref[:, HD:] = keys
        v2_ref[:, :HD] = values

    load(k_ref[0], v_ref[0])

    per = BLOCK // 8
    kept_row = kept_ref[pl.ds(core[0], 1), pl.ds(pl.multiple_of(step * per, per), per)] - step * BLOCK
    lane = lax.broadcasted_iota(jnp.int32, (slots, PICK), 1)
    for half in range(per // LANES):
        col = jnp.transpose(jnp.broadcast_to(kept_row[:, half * LANES : (half + 1) * LANES], (LANES, LANES)))[:, :1]
        for piece in range(LANES // slots):
            at = (half * LANES + piece * slots) * 8
            hot = jnp.where(lane == col[piece * slots : (piece + 1) * slots, :] - at, 1.0, 0.0).astype(bf16)
            both = jnp.concatenate([k_ref[0, at : at + PICK, :], v_ref[0, at : at + PICK, :]], axis=1)
            got = dot(hot, both).astype(bf16)
            here = pl.ds(half * LANES + piece * slots, slots)
            kk_ref[here, :] = got[:, :HD]
            kv_ref[here, :] = got[:, HD:]

    def scores_of(tile, base, masked):
        scores = dot(q2_ref[pl.ds(tile * ROWS, ROWS), :], k2_ref[...], NT)
        if masked:
            cols = columns_of(pos_ref[...]) - base
            pos = stack_columns(cols, tile * ROWS // LANES, ROWS // LANES)
            lane = lax.broadcasted_iota(jnp.int32, scores.shape, 1)
            scores = jnp.where(lane <= pos, scores, -jnp.inf)
        return scores

    def go(first, masked):
        for tile in range(tiles):
            here = pl.ds(tile * ROWS, ROWS)
            scores = scores_of(tile, step * BLOCK, masked)
            if first:
                m_ref[here, :] = jnp.broadcast_to(jnp.max(scores, axis=1, keepdims=True), (ROWS, LANES))
            expo = jnp.exp2(scores - m_ref[here, :1]).astype(bf16)
            acc_ref[here, :] += dot(expo, v2_ref[...])

    half = steps // 2

    @pl.when(step == 0)
    def _():
        go(True, False)

    @pl.when((step > 0) & (step < half))
    def _():
        go(False, False)

    @pl.when(step >= half)
    def _():
        go(False, True)

    @pl.when((step == steps - 1) & jnp.logical_not(jnp.max(acc_ref[:, HD:]) <= LIMIT))
    def _():
        m_ref[...] = jnp.full(m_ref.shape, -jnp.inf, f32)
        acc_ref[...] = jnp.zeros(acc_ref.shape, f32)

        def block(j, carry):
            here = pl.ds(pl.multiple_of(j * BLOCK, BLOCK), BLOCK)
            for any_ref, to in ((k_any, k2_ref.at[:, :HD]), (k_any, k2_ref.at[:, HD:]), (v_any, v2_ref.at[:, :HD])):
                copy = pltpu.make_async_copy(any_ref.at[core[0], here, :], to, sem)
                copy.start()
                copy.wait()
            for tile in range(tiles):
                rows_here = pl.ds(tile * ROWS, ROWS)
                scores = scores_of(tile, j * BLOCK, True)
                old = m_ref[rows_here, :]
                new = jnp.maximum(old, jnp.max(scores, axis=1, keepdims=True))
                m_ref[rows_here, :] = new
                expo = jnp.exp2(scores - new[:, :1]).astype(bf16)
                fade = jnp.exp2(old - new)
                both = jnp.concatenate([fade, fade], axis=1)
                acc_ref[rows_here, :] = acc_ref[rows_here, :] * both + dot(expo, v2_ref[...])
            return carry

        lax.fori_loop(0, steps, block, 0)

    @pl.when(step == steps - 1)
    def _():
        t_ref[...] = acc_ref[:, :HD] / acc_ref[:, HD:]


def attend(core, packed, other, kept, keys, values):
    own = packed.shape[1] - packed.shape[1] % LANES
    rows = 2 * own
    steps = keys.shape[1] // BLOCK
    count = kept.shape[1]
    per = BLOCK // 8
    return pl.pallas_call(
        attend_kernel,
        grid_spec=pltpu.PrefetchScalarGridSpec(
            num_scalar_prefetch=1,
            grid=(steps,),
            in_specs=[
                pl.BlockSpec((1,) + packed.shape[1:], lambda j, c: (c[0], 0, 0)),
                whole(other.shape),
                whole(kept.shape),
                pl.BlockSpec((1, BLOCK, HD), lambda j, c: (c[0], j, 0)),
                pl.BlockSpec((1, BLOCK, HD), lambda j, c: (c[0], j, 0)),
                pl.BlockSpec(memory_space=pl.ANY),
                pl.BlockSpec(memory_space=pl.ANY),
            ],
            out_specs=[
                whole((rows, HD)),
                whole((rows, 2 * HD)),
                whole((rows // LANES, LANES)),
                pl.BlockSpec((per, HD), lambda j, c: (j, 0)),
                pl.BlockSpec((per, HD), lambda j, c: (j, 0)),
            ],
            scratch_shapes=[
                pltpu.VMEM((rows, LANES), f32),
                pltpu.VMEM((rows, 2 * HD), f32),
                pltpu.VMEM((BLOCK, 2 * HD), bf16),
                pltpu.VMEM((BLOCK, 2 * HD), bf16),
                pltpu.SemaphoreType.DMA,
            ],
        ),
        out_shape=[
            jax.ShapeDtypeStruct((rows, HD), f32),
            jax.ShapeDtypeStruct((rows, 2 * HD), bf16),
            jax.ShapeDtypeStruct((rows // LANES, LANES), f32),
            jax.ShapeDtypeStruct((count, HD), bf16),
            jax.ShapeDtypeStruct((count, HD), bf16),
        ],
        compiler_params=params(),
        name="attend",
    )(core, packed, other, kept, keys, values, keys, values)


def add_chunks(z_ref, part, first):
    for chunk in range(z_ref.shape[0]):
        cut = part[:, chunk * LANES : (chunk + 1) * LANES]
        z_ref[chunk] = cut if first else z_ref[chunk] + cut


def first_and_rest(tile, body):
    @pl.when(tile == 0)
    def _():
        body(True)

    @pl.when(tile > 0)
    def _():
        body(False)


def start_kernel(core, q2_ref, pos_ref, kept_ref, kk_ref, kv_ref, t_ref, e_ref, over_ref, z_ref, k2_ref):
    tile = pl.program_id(0)

    @pl.when(tile == 0)
    def _():
        k2_ref[:, :HD] = kk_ref[...]
        k2_ref[:, HD:] = kk_ref[...]

    scores = dot(q2_ref[...], k2_ref[...], NT)
    pos = stack_columns(columns_of(pos_ref[...]), 0, ROWS // LANES)
    scores = jnp.where(kept_ref[pl.ds(core[0], 1), :] <= pos, scores, -jnp.inf)
    expo = jnp.exp2(scores - jnp.max(scores, axis=1, keepdims=True))
    over = 1.0 / jnp.sum(expo, axis=1, keepdims=True)
    high, low = halves(expo)
    e_ref[...] = high
    gap = t_ref[...] - (dot(high, kv_ref[...]) + dot(low, kv_ref[...])) * over
    over_ref[...] = jnp.transpose(jnp.broadcast_to(over, (ROWS, LANES)))[:8, :]
    gap_t = stacked(jnp.transpose(gap * over))

    def body(first):
        two = dot(gap_t, high)
        add_chunks(z_ref, two[:HD] + two[HD:] + dot(gap_t[:HD], low), first)

    first_and_rest(tile, body)


def start(core, q2, pos, kept, kept_keys, kept_values, target):
    rows = q2.shape[0]
    count = kept_keys.shape[0]
    return pl.pallas_call(
        start_kernel,
        grid_spec=pltpu.PrefetchScalarGridSpec(
            num_scalar_prefetch=1,
            grid=(rows // ROWS,),
            in_specs=[
                pl.BlockSpec((ROWS, 2 * HD), lambda i, c: (i, 0)),
                pl.BlockSpec((None, ROWS // LANES, LANES), lambda i, c: (i, 0, 0)),
                whole(kept.shape),
                whole((count, HD)),
                whole((count, HD)),
                pl.BlockSpec((ROWS, HD), lambda i, c: (i, 0)),
            ],
            out_specs=[
                pl.BlockSpec((ROWS, count), lambda i, c: (i, 0)),
                pl.BlockSpec((8, ROWS), lambda i, c: (0, i)),
                whole((count // LANES, HD, LANES)),
            ],
            scratch_shapes=[pltpu.VMEM((count, 2 * HD), bf16)],
        ),
        out_shape=[
            jax.ShapeDtypeStruct((rows, count), bf16),
            jax.ShapeDtypeStruct((8, rows), f32),
            jax.ShapeDtypeStruct((count // LANES, HD, LANES), f32),
        ],
        compiler_params=params(),
        name="start",
    )(core, q2, pos.reshape(rows // ROWS, ROWS // LANES, LANES), kept, kept_keys, kept_values, target)


def load_vector(vec_ref, two_ref):
    for chunk in range(vec_ref.shape[0]):
        two_ref[:, chunk * LANES : (chunk + 1) * LANES] = stacked(vec_ref[chunk])


def normal_kernel(vec_ref, e_ref, over_ref, z_ref, two_ref):
    tile = pl.program_id(0)

    @pl.when(tile == 0)
    def _():
        load_vector(vec_ref, two_ref)

    expo = e_ref[...]
    over = over_ref[:1, :]
    two = dot(two_ref[...], expo, NT)
    image = stacked((two[:HD] + two[HD:]) * (over * over))

    def body(first):
        back = dot(image, expo)
        add_chunks(z_ref, back[:HD] + back[HD:], first)

    first_and_rest(tile, body)


def square_kernel(vec_ref, e_ref, over_ref, sums_ref, s_ref, two_ref, total_ref):
    tile = pl.program_id(0)

    @pl.when(tile == 0)
    def _():
        load_vector(vec_ref, two_ref)
        total_ref[...] = jnp.zeros(total_ref.shape, f32)

    two = dot(two_ref[...], e_ref[...], NT)
    image = (two[:HD] + two[HD:]) * over_ref[:1, :]
    total_ref[...] += jnp.sum(image * image, axis=0, keepdims=True)

    @pl.when(tile == pl.num_programs(0) - 1)
    def _():
        last = total_ref[...]
        last = sum(last[:, i * LANES : (i + 1) * LANES] for i in range(ROWS // LANES))
        row = lax.broadcasted_iota(jnp.int32, sums_ref.shape, 0)
        lane = lax.broadcasted_iota(jnp.int32, sums_ref.shape, 1)
        sums = jnp.sum(jnp.where(row == 3, last, sums_ref[...]), axis=1, keepdims=True)
        line = jnp.sum(jnp.where(row == lane, sums, 0.0), axis=0, keepdims=True)
        s_ref[...] = jnp.broadcast_to(line[None], s_ref.shape)


def with_weights(kernel, name, out, vec, expo, over, *more, scratch=()):
    rows, count = expo.shape
    return pl.pallas_call(
        kernel,
        grid=(rows // ROWS,),
        in_specs=[
            whole(vec.shape),
            pl.BlockSpec((ROWS, count), lambda i: (i, 0)),
            pl.BlockSpec((8, ROWS), lambda i: (0, i)),
        ]
        + [whole(a.shape) for a in more],
        out_specs=whole(out),
        out_shape=jax.ShapeDtypeStruct(out, f32),
        scratch_shapes=[pltpu.VMEM((2 * HD, count), bf16), *scratch],
        compiler_params=params(),
        name=name,
    )(vec, expo, over, *more)


def fold_kernel(parts_ref, chunk_ref, copies_ref):
    total = jnp.sum(parts_ref[...], axis=0)
    chunk_ref[...] = total
    copies_ref[...] = jnp.broadcast_to(total[None], copies_ref.shape)


def fold(parts):
    return pl.pallas_call(
        fold_kernel,
        in_specs=[whole(parts.shape)],
        out_specs=[whole(parts.shape[1:]), whole(parts.shape)],
        out_shape=[jax.ShapeDtypeStruct(parts.shape[1:], f32), jax.ShapeDtypeStruct(parts.shape, f32)],
        compiler_params=params(),
        name="fold",
    )(parts)


def fold_image_kernel(ridge, core, parts_ref, res_ref, copies_ref, sums_ref, keep_ref, send_ref, turn_ref):
    res = res_ref[...]
    total = jnp.sum(parts_ref[...], axis=0) + ridge * res
    copies_ref[...] = jnp.broadcast_to(total[None], copies_ref.shape)
    sums_ref[...] = jnp.zeros(sums_ref.shape, f32)
    sums_ref[0:1, :] = jnp.sum(res * res, axis=0, keepdims=True)
    sums_ref[1:2, :] = jnp.sum(res * total, axis=0, keepdims=True)
    sums_ref[2:3, :] = jnp.sum(total * total, axis=0, keepdims=True)
    half = keep_ref.shape[1]
    for i, chunk in enumerate((res, total)):
        turn_ref[...] = jnp.transpose(chunk)
        keep_ref[i] = turn_ref[pl.ds(pl.multiple_of(core[0] * half, half), half), :]
        send_ref[i] = turn_ref[pl.ds(pl.multiple_of((1 - core[0]) * half, half), half), :]


def fold_image(core, ridge, parts, res):
    half = (2, parts.shape[2] // 2, HD)
    return pl.pallas_call(
        lambda *refs: fold_image_kernel(ridge, *refs),
        grid_spec=pltpu.PrefetchScalarGridSpec(
            num_scalar_prefetch=1,
            grid=(1,),
            in_specs=[whole(parts.shape), whole(res.shape)],
            out_specs=[whole(parts.shape), whole((8, LANES)), whole(half), whole(half)],
            scratch_shapes=[pltpu.VMEM(res.shape, f32)],
        ),
        out_shape=[
            jax.ShapeDtypeStruct(parts.shape, f32),
            jax.ShapeDtypeStruct((8, LANES), f32),
            jax.ShapeDtypeStruct(half, f32),
            jax.ShapeDtypeStruct(half, f32),
        ],
        compiler_params=params(),
        name="fold_image",
    )(core, parts, res)


def finish_kernel(ridge, core, sums_ref, keep_ref, got_ref, out_ref):
    sums = jnp.sum(sums_ref[...], axis=0)
    lane = lax.broadcasted_iota(jnp.int32, sums.shape, 1)
    rr, rn, nn, ww = (jnp.sum(jnp.where(lane == i, sums, 0.0), axis=1, keepdims=True) for i in range(4))
    alpha = rr / rn
    new = rr - 2.0 * alpha * rn + alpha * alpha * nn
    beta = new / rr
    grow = 1.0 + beta
    curve = grow * grow * rn - 2.0 * alpha * grow * nn + alpha * alpha * (ww + ridge * nn)
    step = new / curve
    left = alpha + step * grow
    right = -step * alpha
    out_ref[core[0]] = left * keep_ref[0] + right * keep_ref[1]
    out_ref[1 - core[0]] = left * got_ref[0] + right * got_ref[1]


def finish(core, ridge, sums, keep, got):
    return pl.pallas_call(
        lambda *refs: finish_kernel(ridge, *refs),
        grid_spec=pltpu.PrefetchScalarGridSpec(
            num_scalar_prefetch=1,
            grid=(1,),
            in_specs=[whole(sums.shape), whole(keep.shape), whole(got.shape)],
            out_specs=whole(keep.shape),
        ),
        out_shape=jax.ShapeDtypeStruct(keep.shape, f32),
        compiler_params=params(),
        name="finish",
    )(core, sums, keep, got)


def local(history_keys, history_values, queries, positions, kept_index):
    count = kept_index.shape[1]
    own_rows = queries.shape[1]
    devices = lax.axis_size("probe")
    chips = devices // 2
    everyone = lax.axis_size("head") * devices
    ridge = own_rows * devices / (count * count)
    index = lax.rem(lax.axis_index("probe"), 2)
    core = index.astype(jnp.int32).reshape(1)
    swap = [(i, i ^ 1) for i in range(devices)]
    groups = [[2 * i + c for i in range(chips)] for c in range(2)]

    scaled = queries.astype(f32) * (math.log2(math.e) / math.sqrt(HD))
    packed = jnp.concatenate([scaled, positions.astype(f32).reshape(2, own_rows // LANES, LANES)], axis=1)
    other = lax.ppermute(lax.dynamic_index_in_dim(packed, 1 - index, 0, keepdims=False), "probe", swap)
    target, q2, pos, kept_keys, kept_values = attend(core, packed, other, kept_index, history_keys, history_values)
    expo, over, z = start(core, q2, pos, kept_index, kept_keys, kept_values, target)

    def exchange(chunks):
        return lax.all_to_all(chunks, "probe", 0, 0, axis_index_groups=groups, tiled=True)

    res, copies = fold(exchange(z))
    z = with_weights(normal_kernel, "normal", z.shape, exchange(copies), expo, over)
    copies, sums, keep, send = fold_image(core, ridge, exchange(z), res)
    got = lax.ppermute(send, "probe", swap)
    sums = with_weights(
        square_kernel, "square", (everyone, 1, LANES), exchange(copies), expo, over, sums, scratch=[pltpu.VMEM((1, ROWS), f32)]
    )
    sums = lax.all_to_all(sums, ("head", "probe"), 0, 0, tiled=True)
    return finish(core, ridge, sums, keep, got)


def solution(mesh):
    return jax.shard_map(
        local,
        mesh=mesh,
        in_specs=(
            P("head", None, None),
            P("head", None, None),
            P("head", "probe", None),
            P("head", "probe"),
            P("head", None),
        ),
        out_specs=P("head", "probe", None),
        check_vma=False,
    )
```

```python
import math

import jax
import jax.numpy as jnp
from jax import lax
from jax.experimental import pallas as pl
from jax.experimental.pallas import tpu as pltpu
from jax.sharding import Mesh
from jax.sharding import PartitionSpec as P

HD = 128
LANES = 128
BLOCK = 2048
ROWS = 256
PICK = 256
LIMIT = 2.0**40
MIB = 1024 * 1024
START = 32
WEIGHTS = 16
f32 = jnp.float32
bf16 = jnp.bfloat16
NT = (((1,), (1,)), ((), ()))
NN = (((1,), (0,)), ((), ()))


def dot(left, right, dims=NN):
    return lax.dot_general(left, right, dims, preferred_element_type=f32)


def halves(wide):
    high = wide.astype(bf16)
    return high, (wide - high.astype(f32)).astype(bf16)


def stacked(wide):
    return jnp.concatenate(halves(wide), axis=0)


def whole(shape):
    return pl.BlockSpec(shape, lambda *ids: (0,) * len(shape))


def params(mib):
    return pltpu.CompilerParams(vmem_limit_bytes=mib * MIB)


def columns_of(rows):
    return jnp.transpose(rows).astype(jnp.int32)


def stack_columns(cols, first, count):
    return jnp.concatenate([cols[:, i : i + 1] for i in range(first, first + count)], axis=0)


def attend_kernel(core, mine_ref, other_ref, kept_ref, k_any, v_any, t_ref, q2_ref, pos_ref, kk_ref, kv_ref, m_ref, acc_ref, k2_ref, v2_ref, k_buf, v_buf, sem):
    step = pl.program_id(0)
    steps = pl.num_programs(0)
    rows = q2_ref.shape[0]
    own = rows // 2
    tiles = rows // ROWS
    slots = PICK // 8
    slot = lax.rem(step, 2)

    def copies(j, to):
        here = pl.ds(pl.multiple_of(j * BLOCK, BLOCK), BLOCK)
        return (
            pltpu.make_async_copy(k_any.at[core[0], here, :], k_buf.at[to], sem.at[0, to]),
            pltpu.make_async_copy(v_any.at[core[0], here, :], v_buf.at[to], sem.at[1, to]),
        )

    def fetch(j, to):
        for copy in copies(j, to):
            copy.start()

    def arrive(j, to):
        for copy in copies(j, to):
            copy.wait()

    @pl.when(step == 0)
    def _():
        fetch(0, 0)
        for part, ref in enumerate((mine_ref.at[0], other_ref)):
            high, low = halves(ref[:own, :])
            q2_ref[pl.ds(part * own, own), :HD] = high
            q2_ref[pl.ds(part * own, own), HD:] = low
            pos_ref[pl.ds(part * own // LANES, own // LANES), :] = ref[own:, :]
        m_ref[...] = jnp.full(m_ref.shape, -jnp.inf, f32)
        acc_ref[...] = jnp.zeros(acc_ref.shape, f32)
        v2_ref[:, HD:] = jnp.ones((BLOCK, HD), bf16)

    @pl.when(step + 1 < steps)
    def _():
        fetch(step + 1, 1 - slot)

    arrive(step, slot)

    def load(of):
        k2_ref[:, :HD] = k_buf[of]
        k2_ref[:, HD:] = k_buf[of]
        v2_ref[:, :HD] = v_buf[of]

    def pick():
        per = BLOCK // 8
        kept_row = kept_ref[pl.ds(core[0], 1), pl.ds(pl.multiple_of(step * per, per), per)] - step * BLOCK
        lane = lax.broadcasted_iota(jnp.int32, (slots, PICK), 1)
        for half in range(per // LANES):
            col = jnp.transpose(jnp.broadcast_to(kept_row[:, half * LANES : (half + 1) * LANES], (LANES, LANES)))[:, :1]
            for piece in range(LANES // slots):
                at = (half * LANES + piece * slots) * 8
                hot = jnp.where(lane == col[piece * slots : (piece + 1) * slots, :] - at, 1.0, 0.0).astype(bf16)
                both = jnp.concatenate([k_buf[slot, at : at + PICK, :], v_buf[slot, at : at + PICK, :]], axis=1)
                got = dot(hot, both).astype(bf16)
                here = pl.ds(half * LANES + piece * slots, slots)
                kk_ref[here, :] = got[:, :HD]
                kv_ref[here, :] = got[:, HD:]

    def scores_of(tile, base, masked):
        scores = dot(q2_ref[pl.ds(tile * ROWS, ROWS), :], k2_ref[...], NT)
        if masked:
            cols = columns_of(pos_ref[...]) - base
            pos = stack_columns(cols, tile * ROWS // LANES, ROWS // LANES)
            lane = lax.broadcasted_iota(jnp.int32, scores.shape, 1)
            scores = jnp.where(lane <= pos, scores, -jnp.inf)
        return scores

    def tile_now(tile, base, masked, running):
        here = pl.ds(tile * ROWS, ROWS)
        scores = scores_of(tile, base, masked)
        if not running:
            expo = jnp.exp2(scores - m_ref[here, :1]).astype(bf16)
            acc_ref[here, :] += dot(expo, v2_ref[...])
            return
        old = m_ref[here, :]
        new = jnp.maximum(old, jnp.max(scores, axis=1, keepdims=True))
        m_ref[here, :] = new
        expo = jnp.exp2(scores - new[:, :1]).astype(bf16)
        fade = jnp.exp2(old - new)
        both = jnp.concatenate([fade, fade], axis=1)
        acc_ref[here, :] = acc_ref[here, :] * both + dot(expo, v2_ref[...])

    def go(masked, running):
        load(slot)
        for tile in range(tiles):
            tile_now(tile, step * BLOCK, masked, running)
        pick()

    early = step < steps // 2
    follow = (step == 0) | (core[0] == 0)
    for masked in (False, True):
        for running in (False, True):

            @pl.when((early != masked) & (follow == running))
            def _(masked=masked, running=running):
                go(masked, running)

    @pl.when((step == steps - 1) & jnp.logical_not(jnp.max(jnp.max(acc_ref[:, HD : HD + 1], axis=0, keepdims=True)) <= LIMIT))
    def _():
        m_ref[...] = jnp.full(m_ref.shape, -jnp.inf, f32)
        acc_ref[...] = jnp.zeros(acc_ref.shape, f32)

        def block(j, carry):
            fetch(j, 0)
            arrive(j, 0)
            load(0)
            for tile in range(tiles):
                tile_now(tile, j * BLOCK, True, True)
            return carry

        lax.fori_loop(0, steps, block, 0)

    @pl.when(step == steps - 1)
    def _():
        t_ref[...] = acc_ref[:, :HD] / acc_ref[:, HD:]


def attend(core, packed, other, kept, keys, values):
    own = packed.shape[1] - packed.shape[1] % LANES
    rows = 2 * own
    steps = keys.shape[1] // BLOCK
    count = kept.shape[1]
    per = BLOCK // 8
    return pl.pallas_call(
        attend_kernel,
        grid_spec=pltpu.PrefetchScalarGridSpec(
            num_scalar_prefetch=1,
            grid=(steps,),
            in_specs=[
                pl.BlockSpec((1,) + packed.shape[1:], lambda j, c: (c[0], 0, 0)),
                whole(other.shape),
                whole(kept.shape),
                pl.BlockSpec(memory_space=pltpu.HBM),
                pl.BlockSpec(memory_space=pltpu.HBM),
            ],
            out_specs=[
                whole((rows, HD)),
                whole((rows, 2 * HD)),
                whole((rows // LANES, LANES)),
                pl.BlockSpec((per, HD), lambda j, c: (j, 0)),
                pl.BlockSpec((per, HD), lambda j, c: (j, 0)),
            ],
            scratch_shapes=[
                pltpu.VMEM((rows, LANES), f32),
                pltpu.VMEM((rows, 2 * HD), f32),
                pltpu.VMEM((BLOCK, 2 * HD), bf16),
                pltpu.VMEM((BLOCK, 2 * HD), bf16),
                pltpu.VMEM((2, BLOCK, HD), bf16),
                pltpu.VMEM((2, BLOCK, HD), bf16),
                pltpu.SemaphoreType.DMA((2, 2)),
            ],
        ),
        out_shape=[
            jax.ShapeDtypeStruct((rows, HD), f32),
            jax.ShapeDtypeStruct((rows, 2 * HD), bf16),
            jax.ShapeDtypeStruct((rows // LANES, LANES), f32),
            jax.ShapeDtypeStruct((count, HD), bf16),
            jax.ShapeDtypeStruct((count, HD), bf16),
        ],
        compiler_params=params(40),
        name="attend",
    )(core, packed, other, kept, keys, values)


def put_chunks(z_ref, rows):
    for chunk in range(z_ref.shape[0]):
        z_ref[chunk] = rows[:, chunk * LANES : (chunk + 1) * LANES]


def pulled(two, expo):
    back = dot(two, expo)
    return back[:HD] + back[HD:]


def start_kernel(core, q2_ref, pos_ref, kept_ref, kk_ref, kv_ref, t_ref, e_hbm, over_ref, z_ref, e_ref, low_ref, two_ref, sem):
    keys = kk_ref[...]
    keys = jnp.concatenate([keys, keys], axis=1)
    kept = kept_ref[pl.ds(core[0], 1), :]
    cols = columns_of(pos_ref[...])
    for tile in range(e_ref.shape[0] // ROWS):
        here = pl.ds(tile * ROWS, ROWS)
        scores = dot(q2_ref[here, :], keys, NT)
        pos = stack_columns(cols, tile * ROWS // LANES, ROWS // LANES)
        scores = jnp.where(kept <= pos, scores, -jnp.inf)
        expo = jnp.exp2(scores - jnp.max(scores, axis=1, keepdims=True))
        over = 1.0 / jnp.sum(expo, axis=1, keepdims=True)
        high, low = halves(expo)
        e_ref[here, :] = high
        low_ref[here, :] = low
        pltpu.make_async_copy(e_ref.at[here, :], e_hbm.at[here, :], sem.at[tile]).start()
        gap = t_ref[here, :] - (dot(high, kv_ref[...]) + dot(low, kv_ref[...])) * over
        over_ref[:, here] = jnp.transpose(jnp.broadcast_to(over, (ROWS, LANES)))[:8, :]
        two_ref[:, here] = stacked(jnp.transpose(gap * over))
    put_chunks(z_ref, pulled(two_ref[...], e_ref[...]) + dot(two_ref[:HD, :], low_ref[...]))
    for tile in range(e_ref.shape[0] // ROWS):
        here = pl.ds(tile * ROWS, ROWS)
        pltpu.make_async_copy(e_ref.at[here, :], e_hbm.at[here, :], sem.at[tile]).wait()


def start(core, q2, pos, kept, kept_keys, kept_values, target):
    rows = q2.shape[0]
    count = kept_keys.shape[0]
    inputs = (q2, pos, kept, kept_keys, kept_values, target)
    return pl.pallas_call(
        start_kernel,
        grid_spec=pltpu.PrefetchScalarGridSpec(
            num_scalar_prefetch=1,
            grid=(1,),
            in_specs=[whole(x.shape) for x in inputs],
            out_specs=[
                pl.BlockSpec(memory_space=pltpu.HBM),
                whole((8, rows)),
                whole((count // LANES, HD, LANES)),
            ],
            scratch_shapes=[
                pltpu.VMEM((rows, count), bf16),
                pltpu.VMEM((rows, count), bf16),
                pltpu.VMEM((2 * HD, rows), bf16),
                pltpu.SemaphoreType.DMA((rows // ROWS,)),
            ],
        ),
        out_shape=[
            jax.ShapeDtypeStruct((rows, count), bf16),
            jax.ShapeDtypeStruct((8, rows), f32),
            jax.ShapeDtypeStruct((count // LANES, HD, LANES), f32),
        ],
        compiler_params=params(START),
        name="start",
    )(core, *inputs)


def load_vector(vec_ref, two_ref):
    for chunk in range(vec_ref.shape[0]):
        two_ref[:, chunk * LANES : (chunk + 1) * LANES] = stacked(vec_ref[chunk])


def tiles_of(e_hbm, e_ref, sem):
    copies = []
    for tile in range(e_ref.shape[0] // ROWS):
        here = pl.ds(tile * ROWS, ROWS)
        copies.append((here, pltpu.make_async_copy(e_hbm.at[here, :], e_ref.at[here, :], sem.at[tile])))
    for _, copy in copies:
        copy.start()
    return copies


def pushed(vec_ref, here, e_ref):
    two = dot(vec_ref[...], e_ref[here, :], NT)
    return two[:HD] + two[HD:]


def normal_kernel(vec_ref, over_ref, e_hbm, z_ref, two_ref, e_ref, sem, image_ref):
    copies = tiles_of(e_hbm, e_ref, sem)
    load_vector(vec_ref, two_ref)
    for here, copy in copies:
        copy.wait()
        over = over_ref[:1, here]
        image_ref[:, here] = stacked(pushed(two_ref, here, e_ref) * (over * over))
    put_chunks(z_ref, pulled(image_ref[...], e_ref[...]))


def square_kernel(vec_ref, over_ref, e_hbm, sums_ref, s_ref, two_ref, e_ref, sem):
    copies = tiles_of(e_hbm, e_ref, sem)
    load_vector(vec_ref, two_ref)
    total = jnp.zeros((1, ROWS), f32)
    for here, copy in copies:
        copy.wait()
        image = pushed(two_ref, here, e_ref) * over_ref[:1, here]
        total += jnp.sum(image * image, axis=0, keepdims=True)
    last = sum(total[:, i * LANES : (i + 1) * LANES] for i in range(ROWS // LANES))
    row = lax.broadcasted_iota(jnp.int32, sums_ref.shape, 0)
    lane = lax.broadcasted_iota(jnp.int32, sums_ref.shape, 1)
    sums = jnp.sum(jnp.where(row == 3, last, sums_ref[...]), axis=1, keepdims=True)
    line = jnp.sum(jnp.where(row == lane, sums, 0.0), axis=0, keepdims=True)
    s_ref[...] = jnp.broadcast_to(line[None], s_ref.shape)


def with_weights(kernel, name, out, vec, over, expo, *more, scratch=()):
    rows, count = expo.shape
    return pl.pallas_call(
        kernel,
        in_specs=[whole(vec.shape), whole(over.shape), pl.BlockSpec(memory_space=pltpu.HBM)] + [whole(a.shape) for a in more],
        out_specs=whole(out),
        out_shape=jax.ShapeDtypeStruct(out, f32),
        scratch_shapes=[
            pltpu.VMEM((2 * HD, count), bf16),
            pltpu.VMEM((rows, count), bf16),
            pltpu.SemaphoreType.DMA((rows // ROWS,)),
            *scratch,
        ],
        compiler_params=params(WEIGHTS),
        name=name,
    )(vec, over, expo, *more)


def fold_kernel(parts_ref, chunk_ref, copies_ref):
    total = jnp.sum(parts_ref[...], axis=0)
    chunk_ref[...] = total
    copies_ref[...] = jnp.broadcast_to(total[None], copies_ref.shape)


def fold(parts):
    return pl.pallas_call(
        fold_kernel,
        in_specs=[whole(parts.shape)],
        out_specs=[whole(parts.shape[1:]), whole(parts.shape)],
        out_shape=[jax.ShapeDtypeStruct(parts.shape[1:], f32), jax.ShapeDtypeStruct(parts.shape, f32)],
        compiler_params=params(8),
        name="fold",
    )(parts)


def fold_image_kernel(ridge, core, parts_ref, res_ref, copies_ref, sums_ref, keep_ref, send_ref, turn_ref):
    res = res_ref[...]
    total = jnp.sum(parts_ref[...], axis=0) + ridge * res
    copies_ref[...] = jnp.broadcast_to(total[None], copies_ref.shape)
    sums_ref[...] = jnp.zeros(sums_ref.shape, f32)
    sums_ref[0:1, :] = jnp.sum(res * res, axis=0, keepdims=True)
    sums_ref[1:2, :] = jnp.sum(res * total, axis=0, keepdims=True)
    sums_ref[2:3, :] = jnp.sum(total * total, axis=0, keepdims=True)
    half = keep_ref.shape[1]
    for i, chunk in enumerate((res, total)):
        turn_ref[...] = jnp.transpose(chunk)
        keep_ref[i] = turn_ref[pl.ds(pl.multiple_of(core[0] * half, half), half), :]
        send_ref[i] = turn_ref[pl.ds(pl.multiple_of((1 - core[0]) * half, half), half), :]


def fold_image(core, ridge, parts, res):
    half = (2, parts.shape[2] // 2, HD)
    return pl.pallas_call(
        lambda *refs: fold_image_kernel(ridge, *refs),
        grid_spec=pltpu.PrefetchScalarGridSpec(
            num_scalar_prefetch=1,
            grid=(1,),
            in_specs=[whole(parts.shape), whole(res.shape)],
            out_specs=[whole(parts.shape), whole((8, LANES)), whole(half), whole(half)],
            scratch_shapes=[pltpu.VMEM(res.shape, f32)],
        ),
        out_shape=[
            jax.ShapeDtypeStruct(parts.shape, f32),
            jax.ShapeDtypeStruct((8, LANES), f32),
            jax.ShapeDtypeStruct(half, f32),
            jax.ShapeDtypeStruct(half, f32),
        ],
        compiler_params=params(8),
        name="fold_image",
    )(core, parts, res)


def finish_kernel(ridge, core, sums_ref, keep_ref, got_ref, out_ref):
    sums = jnp.sum(sums_ref[...], axis=0)
    lane = lax.broadcasted_iota(jnp.int32, sums.shape, 1)
    rr, rn, nn, ww = (jnp.sum(jnp.where(lane == i, sums, 0.0), axis=1, keepdims=True) for i in range(4))
    alpha = rr / rn
    new = rr - 2.0 * alpha * rn + alpha * alpha * nn
    beta = new / rr
    grow = 1.0 + beta
    curve = grow * grow * rn - 2.0 * alpha * grow * nn + alpha * alpha * (ww + ridge * nn)
    step = new / curve
    left = alpha + step * grow
    right = -step * alpha
    out_ref[core[0]] = left * keep_ref[0] + right * keep_ref[1]
    out_ref[1 - core[0]] = left * got_ref[0] + right * got_ref[1]


def finish(core, ridge, sums, keep, got):
    return pl.pallas_call(
        lambda *refs: finish_kernel(ridge, *refs),
        grid_spec=pltpu.PrefetchScalarGridSpec(
            num_scalar_prefetch=1,
            grid=(1,),
            in_specs=[whole(sums.shape), whole(keep.shape), whole(got.shape)],
            out_specs=whole(keep.shape),
        ),
        out_shape=jax.ShapeDtypeStruct(keep.shape, f32),
        compiler_params=params(4),
        name="finish",
    )(core, sums, keep, got)


def local(history_keys, history_values, queries, positions, kept_index):
    count = kept_index.shape[1]
    own_rows = queries.shape[1]
    devices = lax.axis_size(("chip", "core"))
    everyone = lax.axis_size("head") * devices
    ridge = own_rows * devices / (count * count)
    index = lax.axis_index("core")
    core = index.astype(jnp.int32).reshape(1)
    swap = [(0, 1), (1, 0)]

    scaled = queries.astype(f32) * (math.log2(math.e) / math.sqrt(HD))
    packed = jnp.concatenate([scaled, positions.astype(f32).reshape(2, own_rows // LANES, LANES)], axis=1)
    other = lax.ppermute(lax.dynamic_index_in_dim(packed, 1 - index, 0, keepdims=False), "core", swap)
    history_keys = pltpu.with_memory_space_constraint(history_keys, pltpu.HBM)
    history_values = pltpu.with_memory_space_constraint(history_values, pltpu.HBM)
    target, q2, pos, kept_keys, kept_values = attend(core, packed, other, kept_index, history_keys, history_values)
    expo, over, z = start(core, q2, pos, kept_index, kept_keys, kept_values, target)

    def exchange(chunks):
        return lax.all_to_all(chunks, "chip", 0, 0, tiled=True)

    res, copies = fold(exchange(z))
    z = with_weights(
        normal_kernel, "normal", z.shape, exchange(copies), over, expo, scratch=[pltpu.VMEM((2 * HD, 2 * own_rows), bf16)]
    )
    copies, sums, keep, send = fold_image(core, ridge, exchange(z), res)
    copies, send = lax.optimization_barrier((exchange(copies), send))
    got = lax.ppermute(send, "core", swap)
    sums = with_weights(square_kernel, "square", (everyone, 1, LANES), copies, over, expo, sums)
    sums = lax.all_to_all(sums, ("head", "chip", "core"), 0, 0, tiled=True)
    return finish(core, ridge, sums, keep, got)


def solution(mesh):
    heads, probes = mesh.devices.shape
    split = Mesh(mesh.devices.reshape(heads, probes // 2, 2), ("head", "chip", "core"))
    probe = ("chip", "core")
    return jax.shard_map(
        local,
        mesh=split,
        in_specs=(
            P("head", None, None),
            P("head", None, None),
            P("head", probe, None),
            P("head", probe),
            P("head", None),
        ),
        out_specs=P("head", probe, None),
        check_vma=False,
    )
```

```python
import math

import jax
import jax.numpy as jnp
from jax import lax
from jax.experimental import pallas as pl
from jax.experimental.pallas import tpu as pltpu
from jax.sharding import Mesh
from jax.sharding import PartitionSpec as P

HD = 128
LANES = 128
BLOCK = 2048
ROWS = 256
PICK = 256
LIMIT = 2.0**40
SCALE = math.log2(math.e) / math.sqrt(HD)
MIB = 1024 * 1024
START = 32
WEIGHTS = 16
f32 = jnp.float32
bf16 = jnp.bfloat16
NT = (((1,), (1,)), ((), ()))
NN = (((1,), (0,)), ((), ()))


def dot(left, right, dims=NN):
    return lax.dot_general(left, right, dims, preferred_element_type=f32)


def halves(wide):
    high = wide.astype(bf16)
    return high, (wide - high.astype(f32)).astype(bf16)


def stacked(wide):
    return jnp.concatenate(halves(wide), axis=0)


def whole(shape):
    return pl.BlockSpec(shape, lambda *ids: (0,) * len(shape))


def params(mib):
    return pltpu.CompilerParams(vmem_limit_bytes=mib * MIB)


def columns_of(rows):
    return jnp.transpose(rows).astype(jnp.int32)


def stack_columns(cols, first, count):
    return jnp.concatenate([cols[:, i : i + 1] for i in range(first, first + count)], axis=0)


def row_of(ref, which, here):
    return jnp.where(which == 0, ref[0:1, here], ref[1:2, here])


def pack_kernel(core, q_ref, place_ref, out_ref):
    own = q_ref.shape[1]
    out_ref[:own, :] = q_ref[1 - core[0]].astype(f32)
    for line in range(own // LANES):
        here = pl.ds(line * LANES, LANES)
        out_ref[own + line : own + line + 1, :] = row_of(place_ref, 1 - core[0], here).astype(f32)
    out_ref[own + own // LANES :, :] = jnp.zeros((8 - own // LANES % 8, LANES), f32)


def pack(core, queries, positions):
    own = queries.shape[1]
    lines = own // LANES
    out = (own + lines + 8 - lines % 8, HD)
    return pl.pallas_call(
        pack_kernel,
        grid_spec=pltpu.PrefetchScalarGridSpec(
            num_scalar_prefetch=1,
            grid=(1,),
            in_specs=[whole(queries.shape), whole(positions.shape)],
            out_specs=whole(out),
        ),
        out_shape=jax.ShapeDtypeStruct(out, f32),
        compiler_params=params(4),
        name="pack",
    )(core, queries, positions)


def attend_kernel(core, mine_ref, place_ref, other_ref, kept_ref, k_any, v_any, t_ref, q_ref, pos_ref, kk_ref, kv_ref, m_ref, acc_ref, v2_ref, k_buf, v_buf, sem):
    step = pl.program_id(0)
    steps = pl.num_programs(0)
    rows = q_ref.shape[0]
    own = rows // 2
    lines = own // LANES
    tiles = rows // ROWS
    slots = PICK // 8
    slot = lax.rem(step, 2)

    def copies(j, to):
        here = pl.ds(pl.multiple_of(j * BLOCK, BLOCK), BLOCK)
        return (
            pltpu.make_async_copy(k_any.at[core[0], here, :], k_buf.at[to], sem.at[0, to]),
            pltpu.make_async_copy(v_any.at[core[0], here, :], v_buf.at[to], sem.at[1, to]),
        )

    def fetch(j, to):
        for copy in copies(j, to):
            copy.start()

    def arrive(j, to):
        for copy in copies(j, to):
            copy.wait()

    @pl.when(step == 0)
    def _():
        fetch(0, 0)
        q_ref[:own, :] = mine_ref[core[0]]
        q_ref[own:, :] = other_ref[:own, :].astype(bf16)
        for line in range(lines):
            here = pl.ds(line * LANES, LANES)
            pos_ref[line : line + 1, :] = row_of(place_ref, core[0], here).astype(f32)
        pos_ref[lines:, :] = other_ref[own : own + lines, :]
        m_ref[...] = jnp.full(m_ref.shape, -jnp.inf, f32)
        acc_ref[...] = jnp.zeros(acc_ref.shape, f32)
        v2_ref[:, HD:] = jnp.ones((BLOCK, HD), bf16)

    @pl.when(step + 1 < steps)
    def _():
        fetch(step + 1, 1 - slot)

    arrive(step, slot)

    def load(of):
        v2_ref[:, :HD] = v_buf[of]

    def pick():
        per = BLOCK // 8
        kept_row = kept_ref[pl.ds(core[0], 1), pl.ds(pl.multiple_of(step * per, per), per)] - step * BLOCK
        lane = lax.broadcasted_iota(jnp.int32, (slots, PICK), 1)
        for half in range(per // LANES):
            col = jnp.transpose(jnp.broadcast_to(kept_row[:, half * LANES : (half + 1) * LANES], (LANES, LANES)))[:, :1]
            for piece in range(LANES // slots):
                at = (half * LANES + piece * slots) * 8
                hot = jnp.where(lane == col[piece * slots : (piece + 1) * slots, :] - at, 1.0, 0.0).astype(bf16)
                both = jnp.concatenate([k_buf[slot, at : at + PICK, :], v_buf[slot, at : at + PICK, :]], axis=1)
                got = dot(hot, both).astype(bf16)
                here = pl.ds(half * LANES + piece * slots, slots)
                kk_ref[here, :] = got[:, :HD]
                kv_ref[here, :] = got[:, HD:]

    def scores_of(tile, of, base, masked):
        scores = dot(q_ref[pl.ds(tile * ROWS, ROWS), :], k_buf[of], NT) * SCALE
        if masked:
            cols = columns_of(pos_ref[...]) - base
            pos = stack_columns(cols, tile * ROWS // LANES, ROWS // LANES)
            lane = lax.broadcasted_iota(jnp.int32, scores.shape, 1)
            scores = jnp.where(lane <= pos, scores, -jnp.inf)
        return scores

    def tile_now(tile, of, base, masked, running):
        here = pl.ds(tile * ROWS, ROWS)
        scores = scores_of(tile, of, base, masked)
        if not running:
            expo = jnp.exp2(scores - m_ref[here, :1]).astype(bf16)
            acc_ref[here, :] += dot(expo, v2_ref[...])
            return
        old = m_ref[here, :]
        new = jnp.maximum(old, jnp.max(scores, axis=1, keepdims=True))
        m_ref[here, :] = new
        expo = jnp.exp2(scores - new[:, :1]).astype(bf16)
        fade = jnp.exp2(old - new)
        both = jnp.concatenate([fade, fade], axis=1)
        acc_ref[here, :] = acc_ref[here, :] * both + dot(expo, v2_ref[...])

    def go(masked, running):
        load(slot)
        for tile in range(tiles):
            tile_now(tile, slot, step * BLOCK, masked, running)
        pick()

    early = step < steps // 2
    follow = (step == 0) | ((core[0] == 0) & (step >= steps // 2))
    for masked in (False, True):
        for running in (False, True):

            @pl.when((early != masked) & (follow == running))
            def _(masked=masked, running=running):
                go(masked, running)

    @pl.when((step == steps - 1) & jnp.logical_not(jnp.max(jnp.max(acc_ref[:, HD : HD + 1], axis=0, keepdims=True)) <= LIMIT))
    def _():
        m_ref[...] = jnp.full(m_ref.shape, -jnp.inf, f32)
        acc_ref[...] = jnp.zeros(acc_ref.shape, f32)

        def block(j, carry):
            fetch(j, 0)
            arrive(j, 0)
            load(0)
            for tile in range(tiles):
                tile_now(tile, 0, j * BLOCK, True, True)
            return carry

        lax.fori_loop(0, steps, block, 0)

    @pl.when(step == steps - 1)
    def _():
        t_ref[...] = acc_ref[:, :HD] / acc_ref[:, HD:]


def attend(core, queries, positions, other, kept, keys, values):
    rows = 2 * queries.shape[1]
    steps = keys.shape[1] // BLOCK
    count = kept.shape[1]
    per = BLOCK // 8
    return pl.pallas_call(
        attend_kernel,
        grid_spec=pltpu.PrefetchScalarGridSpec(
            num_scalar_prefetch=1,
            grid=(steps,),
            in_specs=[
                whole(queries.shape),
                whole(positions.shape),
                whole(other.shape),
                whole(kept.shape),
                pl.BlockSpec(memory_space=pltpu.HBM),
                pl.BlockSpec(memory_space=pltpu.HBM),
            ],
            out_specs=[
                whole((rows, HD)),
                whole((rows, HD)),
                whole((rows // LANES, LANES)),
                pl.BlockSpec((per, HD), lambda j, c: (j, 0)),
                pl.BlockSpec((per, HD), lambda j, c: (j, 0)),
            ],
            scratch_shapes=[
                pltpu.VMEM((rows, LANES), f32),
                pltpu.VMEM((rows, 2 * HD), f32),
                pltpu.VMEM((BLOCK, 2 * HD), bf16),
                pltpu.VMEM((2, BLOCK, HD), bf16),
                pltpu.VMEM((2, BLOCK, HD), bf16),
                pltpu.SemaphoreType.DMA((2, 2)),
            ],
        ),
        out_shape=[
            jax.ShapeDtypeStruct((rows, HD), f32),
            jax.ShapeDtypeStruct((rows, HD), bf16),
            jax.ShapeDtypeStruct((rows // LANES, LANES), f32),
            jax.ShapeDtypeStruct((count, HD), bf16),
            jax.ShapeDtypeStruct((count, HD), bf16),
        ],
        compiler_params=params(40),
        name="attend",
    )(core, queries, positions, other, kept, keys, values)


def put_chunks(z_ref, rows):
    for chunk in range(z_ref.shape[0]):
        z_ref[chunk] = rows[:, chunk * LANES : (chunk + 1) * LANES]


def pulled(two, expo):
    back = dot(two, expo)
    return back[:HD] + back[HD:]


def start_kernel(core, q_ref, pos_ref, kept_ref, kk_ref, kv_ref, t_ref, e_ref, over_ref, z_ref, low_ref, two_ref):
    kept = kept_ref[pl.ds(core[0], 1), :]
    cols = columns_of(pos_ref[...])
    for tile in range(e_ref.shape[0] // ROWS):
        here = pl.ds(tile * ROWS, ROWS)
        scores = dot(q_ref[here, :], kk_ref[...], NT) * SCALE
        pos = stack_columns(cols, tile * ROWS // LANES, ROWS // LANES)
        scores = jnp.where(kept <= pos, scores, -jnp.inf)
        expo = jnp.exp2(scores - jnp.max(scores, axis=1, keepdims=True))
        over = 1.0 / jnp.sum(expo, axis=1, keepdims=True)
        high, low = halves(expo)
        e_ref[here, :] = high
        low_ref[here, :] = low
        gap = t_ref[here, :] - (dot(high, kv_ref[...]) + dot(low, kv_ref[...])) * over
        over_ref[:, here] = jnp.transpose(jnp.broadcast_to(over, (ROWS, LANES)))[:8, :]
        two_ref[:, here] = stacked(jnp.transpose(gap * over))
    put_chunks(z_ref, pulled(two_ref[...], e_ref[...]) + dot(two_ref[:HD, :], low_ref[...]))


def start(core, q, pos, kept, kept_keys, kept_values, target):
    rows = q.shape[0]
    count = kept_keys.shape[0]
    inputs = (q, pos, kept, kept_keys, kept_values, target)
    return pl.pallas_call(
        start_kernel,
        grid_spec=pltpu.PrefetchScalarGridSpec(
            num_scalar_prefetch=1,
            grid=(1,),
            in_specs=[whole(x.shape) for x in inputs],
            out_specs=[
                whole((rows, count)),
                whole((8, rows)),
                whole((count // LANES, HD, LANES)),
            ],
            scratch_shapes=[
                pltpu.VMEM((rows, count), bf16),
                pltpu.VMEM((2 * HD, rows), bf16),
            ],
        ),
        out_shape=[
            jax.ShapeDtypeStruct((rows, count), bf16),
            jax.ShapeDtypeStruct((8, rows), f32),
            jax.ShapeDtypeStruct((count // LANES, HD, LANES), f32),
        ],
        compiler_params=params(START),
        name="start",
    )(core, *inputs)


def load_vector(vec_ref, two_ref):
    for chunk in range(vec_ref.shape[0]):
        two_ref[:, chunk * LANES : (chunk + 1) * LANES] = stacked(vec_ref[chunk])


def tiles_of(e_ref):
    return [pl.ds(tile * ROWS, ROWS) for tile in range(e_ref.shape[0] // ROWS)]


def pushed(vec_ref, here, e_ref):
    two = dot(vec_ref[...], e_ref[here, :], NT)
    return two[:HD] + two[HD:]


def normal_kernel(vec_ref, over_ref, e_ref, z_ref, two_ref, image_ref):
    load_vector(vec_ref, two_ref)
    for here in tiles_of(e_ref):
        over = over_ref[:1, here]
        image_ref[:, here] = stacked(pushed(two_ref, here, e_ref) * (over * over))
    put_chunks(z_ref, pulled(image_ref[...], e_ref[...]))


def square_kernel(vec_ref, over_ref, e_ref, sums_ref, s_ref, two_ref):
    load_vector(vec_ref, two_ref)
    total = jnp.zeros((1, ROWS), f32)
    for here in tiles_of(e_ref):
        image = pushed(two_ref, here, e_ref) * over_ref[:1, here]
        total += jnp.sum(image * image, axis=0, keepdims=True)
    last = sum(total[:, i * LANES : (i + 1) * LANES] for i in range(ROWS // LANES))
    row = lax.broadcasted_iota(jnp.int32, sums_ref.shape, 0)
    lane = lax.broadcasted_iota(jnp.int32, sums_ref.shape, 1)
    sums = jnp.sum(jnp.where(row == 3, last, sums_ref[...]), axis=1, keepdims=True)
    line = jnp.sum(jnp.where(row == lane, sums, 0.0), axis=0, keepdims=True)
    s_ref[...] = jnp.broadcast_to(line[None], s_ref.shape)


def with_weights(kernel, name, out, vec, over, expo, *more, scratch=()):
    rows, count = expo.shape
    return pl.pallas_call(
        kernel,
        in_specs=[whole(vec.shape), whole(over.shape), whole(expo.shape)] + [whole(a.shape) for a in more],
        out_specs=whole(out),
        out_shape=jax.ShapeDtypeStruct(out, f32),
        scratch_shapes=[
            pltpu.VMEM((2 * HD, count), bf16),
            *scratch,
        ],
        compiler_params=params(WEIGHTS),
        name=name,
    )(vec, over, expo, *more)


def fold_kernel(parts_ref, chunk_ref, copies_ref):
    total = jnp.sum(parts_ref[...], axis=0)
    chunk_ref[...] = total
    copies_ref[...] = jnp.broadcast_to(total[None], copies_ref.shape)


def fold(parts):
    return pl.pallas_call(
        fold_kernel,
        in_specs=[whole(parts.shape)],
        out_specs=[whole(parts.shape[1:]), whole(parts.shape)],
        out_shape=[jax.ShapeDtypeStruct(parts.shape[1:], f32), jax.ShapeDtypeStruct(parts.shape, f32)],
        compiler_params=params(8),
        name="fold",
    )(parts)


def fold_image_kernel(ridge, core, parts_ref, res_ref, copies_ref, sums_ref, keep_ref, send_ref, turn_ref):
    res = res_ref[...]
    total = jnp.sum(parts_ref[...], axis=0) + ridge * res
    copies_ref[...] = jnp.broadcast_to(total[None], copies_ref.shape)
    sums_ref[...] = jnp.zeros(sums_ref.shape, f32)
    sums_ref[0:1, :] = jnp.sum(res * res, axis=0, keepdims=True)
    sums_ref[1:2, :] = jnp.sum(res * total, axis=0, keepdims=True)
    sums_ref[2:3, :] = jnp.sum(total * total, axis=0, keepdims=True)
    half = keep_ref.shape[1]
    for i, chunk in enumerate((res, total)):
        turn_ref[...] = jnp.transpose(chunk)
        keep_ref[i] = turn_ref[pl.ds(pl.multiple_of(core[0] * half, half), half), :]
        send_ref[i] = turn_ref[pl.ds(pl.multiple_of((1 - core[0]) * half, half), half), :]


def fold_image(core, ridge, parts, res):
    half = (2, parts.shape[2] // 2, HD)
    return pl.pallas_call(
        lambda *refs: fold_image_kernel(ridge, *refs),
        grid_spec=pltpu.PrefetchScalarGridSpec(
            num_scalar_prefetch=1,
            grid=(1,),
            in_specs=[whole(parts.shape), whole(res.shape)],
            out_specs=[whole(parts.shape), whole((8, LANES)), whole(half), whole(half)],
            scratch_shapes=[pltpu.VMEM(res.shape, f32)],
        ),
        out_shape=[
            jax.ShapeDtypeStruct(parts.shape, f32),
            jax.ShapeDtypeStruct((8, LANES), f32),
            jax.ShapeDtypeStruct(half, f32),
            jax.ShapeDtypeStruct(half, f32),
        ],
        compiler_params=params(8),
        name="fold_image",
    )(core, parts, res)


def finish_kernel(ridge, core, sums_ref, keep_ref, got_ref, out_ref):
    sums = jnp.sum(sums_ref[...], axis=0)
    lane = lax.broadcasted_iota(jnp.int32, sums.shape, 1)
    rr, rn, nn, ww = (jnp.sum(jnp.where(lane == i, sums, 0.0), axis=1, keepdims=True) for i in range(4))
    alpha = rr / rn
    new = rr - 2.0 * alpha * rn + alpha * alpha * nn
    beta = new / rr
    grow = 1.0 + beta
    curve = grow * grow * rn - 2.0 * alpha * grow * nn + alpha * alpha * (ww + ridge * nn)
    step = new / curve
    left = alpha + step * grow
    right = -step * alpha
    out_ref[core[0]] = left * keep_ref[0] + right * keep_ref[1]
    out_ref[1 - core[0]] = left * got_ref[0] + right * got_ref[1]


def finish(core, ridge, sums, keep, got):
    return pl.pallas_call(
        lambda *refs: finish_kernel(ridge, *refs),
        grid_spec=pltpu.PrefetchScalarGridSpec(
            num_scalar_prefetch=1,
            grid=(1,),
            in_specs=[whole(sums.shape), whole(keep.shape), whole(got.shape)],
            out_specs=whole(keep.shape),
        ),
        out_shape=jax.ShapeDtypeStruct(keep.shape, f32),
        compiler_params=params(4),
        name="finish",
    )(core, sums, keep, got)


def local(history_keys, history_values, queries, positions, kept_index):
    count = kept_index.shape[1]
    own_rows = queries.shape[1]
    devices = lax.axis_size(("chip", "core"))
    everyone = lax.axis_size("head") * devices
    ridge = own_rows * devices / (count * count)
    index = lax.axis_index("core")
    core = index.astype(jnp.int32).reshape(1)
    swap = [(0, 1), (1, 0)]

    history_keys, history_values, queries, positions, kept_index = (
        pltpu.with_memory_space_constraint(x, pltpu.HBM)
        for x in (history_keys, history_values, queries, positions, kept_index)
    )

    other = lax.ppermute(pack(core, queries, positions), "core", swap)
    target, q, pos, kept_keys, kept_values = attend(
        core, queries, positions, other, kept_index, history_keys, history_values
    )
    expo, over, z = start(core, q, pos, kept_index, kept_keys, kept_values, target)

    def exchange(chunks):
        return lax.all_to_all(chunks, "chip", 0, 0, tiled=True)

    res, copies = fold(exchange(z))
    z = with_weights(
        normal_kernel, "normal", z.shape, exchange(copies), over, expo, scratch=[pltpu.VMEM((2 * HD, 2 * own_rows), bf16)]
    )
    copies, sums, keep, send = fold_image(core, ridge, exchange(z), res)
    copies, send = lax.optimization_barrier((exchange(copies), send))
    got = lax.ppermute(send, "core", swap)
    sums = with_weights(square_kernel, "square", (everyone, 1, LANES), copies, over, expo, sums)
    sums = lax.all_to_all(sums, ("head", "chip", "core"), 0, 0, tiled=True)
    return finish(core, ridge, sums, keep, got)


def solution(mesh):
    heads, probes = mesh.devices.shape
    split = Mesh(mesh.devices.reshape(heads, probes // 2, 2), ("head", "chip", "core"))
    probe = ("chip", "core")
    return jax.shard_map(
        local,
        mesh=split,
        in_specs=(
            P("head", None, None),
            P("head", None, None),
            P("head", probe, None),
            P("head", probe),
            P("head", None),
        ),
        out_specs=P("head", probe, None),
        check_vma=False,
    )
```

```python
import math

import jax
import jax.numpy as jnp
from jax import lax
from jax.experimental import pallas as pl
from jax.experimental.pallas import tpu as pltpu
from jax.sharding import Mesh
from jax.sharding import PartitionSpec as P

HD = 128
LANES = 128
BLOCK = 2048
ROWS = 256
PICK = 256
LIMIT = 2.0**40
SCALE = math.log2(math.e) / math.sqrt(HD)
MIB = 1024 * 1024
START = 32
WEIGHTS = 16
f32 = jnp.float32
bf16 = jnp.bfloat16
NT = (((1,), (1,)), ((), ()))
NN = (((1,), (0,)), ((), ()))


def dot(left, right, dims=NN):
    return lax.dot_general(left, right, dims, preferred_element_type=f32)


def halves(wide):
    high = wide.astype(bf16)
    return high, (wide - high.astype(f32)).astype(bf16)


def stacked(wide):
    return jnp.concatenate(halves(wide), axis=0)


def whole(shape):
    return pl.BlockSpec(shape, lambda *ids: (0,) * len(shape))


def params(mib):
    return pltpu.CompilerParams(vmem_limit_bytes=mib * MIB)


def columns_of(rows):
    return jnp.transpose(rows).astype(jnp.int32)


def stack_columns(cols, first, count):
    return jnp.concatenate([cols[:, i : i + 1] for i in range(first, first + count)], axis=0)


def row_of(ref, which, here):
    return jnp.where(which == 0, ref[0:1, here], ref[1:2, here])


def pack_kernel(core, q_ref, place_ref, kept_ref, mine_ref, send_ref, kept_out):
    own = q_ref.shape[1]
    lines = own // LANES
    for which, out_ref in ((core[0], mine_ref), (1 - core[0], send_ref)):
        out_ref[:own, :] = q_ref[which].astype(f32)
        for line in range(lines):
            here = pl.ds(line * LANES, LANES)
            out_ref[own + line : own + line + 1, :] = row_of(place_ref, which, here).astype(f32)
        out_ref[own + lines :, :] = jnp.zeros((8 - lines % 8, LANES), f32)
    kept_out[...] = kept_ref[...]


def pack(core, queries, positions, kept):
    own = queries.shape[1]
    lines = own // LANES
    out = (own + lines + 8 - lines % 8, HD)
    return pl.pallas_call(
        pack_kernel,
        grid_spec=pltpu.PrefetchScalarGridSpec(
            num_scalar_prefetch=1,
            grid=(1,),
            in_specs=[whole(queries.shape), whole(positions.shape), whole(kept.shape)],
            out_specs=[whole(out), whole(out), whole(kept.shape)],
        ),
        out_shape=[
            jax.ShapeDtypeStruct(out, f32),
            jax.ShapeDtypeStruct(out, f32),
            jax.ShapeDtypeStruct(kept.shape, jnp.int32),
        ],
        compiler_params=params(4),
        name="pack",
    )(core, queries, positions, kept)


def attend_kernel(core, mine_ref, other_ref, kept_ref, k_any, v_any, t_ref, q_ref, pos_ref, kk_ref, kv_ref, m_ref, acc_ref, v2_ref, k_buf, v_buf, sem):
    step = pl.program_id(0)
    steps = pl.num_programs(0)
    rows = q_ref.shape[0]
    own = rows // 2
    lines = own // LANES
    tiles = rows // ROWS
    slots = PICK // 8
    slot = lax.rem(step, 2)

    def copies(j, to):
        here = pl.ds(pl.multiple_of(j * BLOCK, BLOCK), BLOCK)
        return (
            pltpu.make_async_copy(k_any.at[core[0], here, :], k_buf.at[to], sem.at[0, to]),
            pltpu.make_async_copy(v_any.at[core[0], here, :], v_buf.at[to], sem.at[1, to]),
        )

    def fetch(j, to):
        for copy in copies(j, to):
            copy.start()

    def arrive(j, to):
        for copy in copies(j, to):
            copy.wait()

    @pl.when(step == 0)
    def _():
        fetch(0, 0)
        for part, ref in enumerate((mine_ref, other_ref)):
            q_ref[pl.ds(part * own, own), :] = ref[:own, :].astype(bf16)
            pos_ref[pl.ds(part * lines, lines), :] = ref[own : own + lines, :]
        m_ref[...] = jnp.full(m_ref.shape, -jnp.inf, f32)
        acc_ref[...] = jnp.zeros(acc_ref.shape, f32)
        v2_ref[:, HD:] = jnp.ones((BLOCK, HD), bf16)

    @pl.when(step + 1 < steps)
    def _():
        fetch(step + 1, 1 - slot)

    arrive(step, slot)

    def load(of):
        v2_ref[:, :HD] = v_buf[of]

    def pick():
        per = BLOCK // 8
        kept_row = kept_ref[pl.ds(core[0], 1), pl.ds(pl.multiple_of(step * per, per), per)] - step * BLOCK
        lane = lax.broadcasted_iota(jnp.int32, (slots, PICK), 1)
        for half in range(per // LANES):
            col = jnp.transpose(jnp.broadcast_to(kept_row[:, half * LANES : (half + 1) * LANES], (LANES, LANES)))[:, :1]
            for piece in range(LANES // slots):
                at = (half * LANES + piece * slots) * 8
                hot = jnp.where(lane == col[piece * slots : (piece + 1) * slots, :] - at, 1.0, 0.0).astype(bf16)
                both = jnp.concatenate([k_buf[slot, at : at + PICK, :], v_buf[slot, at : at + PICK, :]], axis=1)
                got = dot(hot, both).astype(bf16)
                here = pl.ds(half * LANES + piece * slots, slots)
                kk_ref[here, :] = got[:, :HD]
                kv_ref[here, :] = got[:, HD:]

    def scores_of(tile, of, base, masked):
        scores = dot(q_ref[pl.ds(tile * ROWS, ROWS), :], k_buf[of], NT) * SCALE
        if masked:
            cols = columns_of(pos_ref[...]) - base
            pos = stack_columns(cols, tile * ROWS // LANES, ROWS // LANES)
            lane = lax.broadcasted_iota(jnp.int32, scores.shape, 1)
            scores = jnp.where(lane <= pos, scores, -jnp.inf)
        return scores

    def tile_now(tile, of, base, masked, running):
        here = pl.ds(tile * ROWS, ROWS)
        scores = scores_of(tile, of, base, masked)
        if not running:
            expo = jnp.exp2(scores - m_ref[here, :1]).astype(bf16)
            acc_ref[here, :] += dot(expo, v2_ref[...])
            return
        old = m_ref[here, :]
        new = jnp.maximum(old, jnp.max(scores, axis=1, keepdims=True))
        m_ref[here, :] = new
        expo = jnp.exp2(scores - new[:, :1]).astype(bf16)
        fade = jnp.exp2(old - new)
        both = jnp.concatenate([fade, fade], axis=1)
        acc_ref[here, :] = acc_ref[here, :] * both + dot(expo, v2_ref[...])

    def go(masked, running):
        load(slot)
        for tile in range(tiles):
            tile_now(tile, slot, step * BLOCK, masked, running)
        pick()

    early = step < steps // 2
    follow = (step == 0) | ((core[0] == 0) & (step >= steps // 2))
    for masked in (False, True):
        for running in (False, True):

            @pl.when((early != masked) & (follow == running))
            def _(masked=masked, running=running):
                go(masked, running)

    @pl.when((step == steps - 1) & jnp.logical_not(jnp.max(jnp.max(acc_ref[:, HD : HD + 1], axis=0, keepdims=True)) <= LIMIT))
    def _():
        m_ref[...] = jnp.full(m_ref.shape, -jnp.inf, f32)
        acc_ref[...] = jnp.zeros(acc_ref.shape, f32)

        def block(j, carry):
            fetch(j, 0)
            arrive(j, 0)
            load(0)
            for tile in range(tiles):
                tile_now(tile, 0, j * BLOCK, True, True)
            return carry

        lax.fori_loop(0, steps, block, 0)

    @pl.when(step == steps - 1)
    def _():
        t_ref[...] = acc_ref[:, :HD] / acc_ref[:, HD:]


def attend(core, mine, other, kept, keys, values):
    rows = 2 * (mine.shape[0] // LANES * LANES)
    steps = keys.shape[1] // BLOCK
    count = kept.shape[1]
    per = BLOCK // 8
    return pl.pallas_call(
        attend_kernel,
        grid_spec=pltpu.PrefetchScalarGridSpec(
            num_scalar_prefetch=1,
            grid=(steps,),
            in_specs=[
                whole(mine.shape),
                whole(other.shape),
                whole(kept.shape),
                pl.BlockSpec(memory_space=pltpu.HBM),
                pl.BlockSpec(memory_space=pltpu.HBM),
            ],
            out_specs=[
                whole((rows, HD)),
                whole((rows, HD)),
                whole((rows // LANES, LANES)),
                pl.BlockSpec((per, HD), lambda j, c: (j, 0)),
                pl.BlockSpec((per, HD), lambda j, c: (j, 0)),
            ],
            scratch_shapes=[
                pltpu.VMEM((rows, LANES), f32),
                pltpu.VMEM((rows, 2 * HD), f32),
                pltpu.VMEM((BLOCK, 2 * HD), bf16),
                pltpu.VMEM((2, BLOCK, HD), bf16),
                pltpu.VMEM((2, BLOCK, HD), bf16),
                pltpu.SemaphoreType.DMA((2, 2)),
            ],
        ),
        out_shape=[
            jax.ShapeDtypeStruct((rows, HD), f32),
            jax.ShapeDtypeStruct((rows, HD), bf16),
            jax.ShapeDtypeStruct((rows // LANES, LANES), f32),
            jax.ShapeDtypeStruct((count, HD), bf16),
            jax.ShapeDtypeStruct((count, HD), bf16),
        ],
        compiler_params=params(40),
        name="attend",
    )(core, mine, other, kept, keys, values)


def put_chunks(z_ref, rows):
    for chunk in range(z_ref.shape[0]):
        z_ref[chunk] = rows[:, chunk * LANES : (chunk + 1) * LANES]


def pulled(two, expo):
    back = dot(two, expo)
    return back[:HD] + back[HD:]


def start_kernel(core, q_ref, pos_ref, kept_ref, kk_ref, kv_ref, t_ref, e_ref, over_ref, z_ref, low_ref, two_ref):
    kept = kept_ref[pl.ds(core[0], 1), :]
    cols = columns_of(pos_ref[...])
    for tile in range(e_ref.shape[0] // ROWS):
        here = pl.ds(tile * ROWS, ROWS)
        scores = dot(q_ref[here, :], kk_ref[...], NT) * SCALE
        pos = stack_columns(cols, tile * ROWS // LANES, ROWS // LANES)
        scores = jnp.where(kept <= pos, scores, -jnp.inf)
        expo = jnp.exp2(scores - jnp.max(scores, axis=1, keepdims=True))
        over = 1.0 / jnp.sum(expo, axis=1, keepdims=True)
        high, low = halves(expo)
        e_ref[here, :] = high
        low_ref[here, :] = low
        gap = t_ref[here, :] - (dot(high, kv_ref[...]) + dot(low, kv_ref[...])) * over
        over_ref[:, here] = jnp.transpose(jnp.broadcast_to(over, (ROWS, LANES)))[:8, :]
        two_ref[:, here] = stacked(jnp.transpose(gap * over))
    put_chunks(z_ref, pulled(two_ref[...], e_ref[...]) + dot(two_ref[:HD, :], low_ref[...]))


def start(core, q, pos, kept, kept_keys, kept_values, target):
    rows = q.shape[0]
    count = kept_keys.shape[0]
    inputs = (q, pos, kept, kept_keys, kept_values, target)
    return pl.pallas_call(
        start_kernel,
        grid_spec=pltpu.PrefetchScalarGridSpec(
            num_scalar_prefetch=1,
            grid=(1,),
            in_specs=[whole(x.shape) for x in inputs],
            out_specs=[
                whole((rows, count)),
                whole((8, rows)),
                whole((count // LANES, HD, LANES)),
            ],
            scratch_shapes=[
                pltpu.VMEM((rows, count), bf16),
                pltpu.VMEM((2 * HD, rows), bf16),
            ],
        ),
        out_shape=[
            jax.ShapeDtypeStruct((rows, count), bf16),
            jax.ShapeDtypeStruct((8, rows), f32),
            jax.ShapeDtypeStruct((count // LANES, HD, LANES), f32),
        ],
        compiler_params=params(START),
        name="start",
    )(core, *inputs)


def load_vector(vec_ref, two_ref):
    for chunk in range(vec_ref.shape[0]):
        two_ref[:, chunk * LANES : (chunk + 1) * LANES] = stacked(vec_ref[chunk])


def tiles_of(e_ref):
    return [pl.ds(tile * ROWS, ROWS) for tile in range(e_ref.shape[0] // ROWS)]


def pushed(vec_ref, here, e_ref):
    two = dot(vec_ref[...], e_ref[here, :], NT)
    return two[:HD] + two[HD:]


def normal_kernel(vec_ref, over_ref, e_ref, z_ref, two_ref, image_ref):
    load_vector(vec_ref, two_ref)
    for here in tiles_of(e_ref):
        over = over_ref[:1, here]
        image_ref[:, here] = stacked(pushed(two_ref, here, e_ref) * (over * over))
    put_chunks(z_ref, pulled(image_ref[...], e_ref[...]))


def square_kernel(vec_ref, over_ref, e_ref, sums_ref, s_ref, two_ref):
    load_vector(vec_ref, two_ref)
    total = jnp.zeros((1, ROWS), f32)
    for here in tiles_of(e_ref):
        image = pushed(two_ref, here, e_ref) * over_ref[:1, here]
        total += jnp.sum(image * image, axis=0, keepdims=True)
    last = sum(total[:, i * LANES : (i + 1) * LANES] for i in range(ROWS // LANES))
    row = lax.broadcasted_iota(jnp.int32, sums_ref.shape, 0)
    lane = lax.broadcasted_iota(jnp.int32, sums_ref.shape, 1)
    sums = jnp.sum(jnp.where(row == 3, last, sums_ref[...]), axis=1, keepdims=True)
    line = jnp.sum(jnp.where(row == lane, sums, 0.0), axis=0, keepdims=True)
    s_ref[...] = jnp.broadcast_to(line[None], s_ref.shape)


def with_weights(kernel, name, out, vec, over, expo, *more, scratch=()):
    rows, count = expo.shape
    return pl.pallas_call(
        kernel,
        in_specs=[whole(vec.shape), whole(over.shape), whole(expo.shape)] + [whole(a.shape) for a in more],
        out_specs=whole(out),
        out_shape=jax.ShapeDtypeStruct(out, f32),
        scratch_shapes=[
            pltpu.VMEM((2 * HD, count), bf16),
            *scratch,
        ],
        compiler_params=params(WEIGHTS),
        name=name,
    )(vec, over, expo, *more)


def fold_kernel(parts_ref, chunk_ref, copies_ref):
    total = jnp.sum(parts_ref[...], axis=0)
    chunk_ref[...] = total
    copies_ref[...] = jnp.broadcast_to(total[None], copies_ref.shape)


def fold(parts):
    return pl.pallas_call(
        fold_kernel,
        in_specs=[whole(parts.shape)],
        out_specs=[whole(parts.shape[1:]), whole(parts.shape)],
        out_shape=[jax.ShapeDtypeStruct(parts.shape[1:], f32), jax.ShapeDtypeStruct(parts.shape, f32)],
        compiler_params=params(8),
        name="fold",
    )(parts)


def fold_image_kernel(ridge, core, parts_ref, res_ref, copies_ref, sums_ref, keep_ref, send_ref, turn_ref):
    res = res_ref[...]
    total = jnp.sum(parts_ref[...], axis=0) + ridge * res
    copies_ref[...] = jnp.broadcast_to(total[None], copies_ref.shape)
    sums_ref[...] = jnp.zeros(sums_ref.shape, f32)
    sums_ref[0:1, :] = jnp.sum(res * res, axis=0, keepdims=True)
    sums_ref[1:2, :] = jnp.sum(res * total, axis=0, keepdims=True)
    sums_ref[2:3, :] = jnp.sum(total * total, axis=0, keepdims=True)
    half = keep_ref.shape[1]
    for i, chunk in enumerate((res, total)):
        turn_ref[...] = jnp.transpose(chunk)
        keep_ref[i] = turn_ref[pl.ds(pl.multiple_of(core[0] * half, half), half), :]
        send_ref[i] = turn_ref[pl.ds(pl.multiple_of((1 - core[0]) * half, half), half), :]


def fold_image(core, ridge, parts, res):
    half = (2, parts.shape[2] // 2, HD)
    return pl.pallas_call(
        lambda *refs: fold_image_kernel(ridge, *refs),
        grid_spec=pltpu.PrefetchScalarGridSpec(
            num_scalar_prefetch=1,
            grid=(1,),
            in_specs=[whole(parts.shape), whole(res.shape)],
            out_specs=[whole(parts.shape), whole((8, LANES)), whole(half), whole(half)],
            scratch_shapes=[pltpu.VMEM(res.shape, f32)],
        ),
        out_shape=[
            jax.ShapeDtypeStruct(parts.shape, f32),
            jax.ShapeDtypeStruct((8, LANES), f32),
            jax.ShapeDtypeStruct(half, f32),
            jax.ShapeDtypeStruct(half, f32),
        ],
        compiler_params=params(8),
        name="fold_image",
    )(core, parts, res)


def finish_kernel(ridge, core, sums_ref, keep_ref, got_ref, out_ref):
    sums = jnp.sum(sums_ref[...], axis=0)
    lane = lax.broadcasted_iota(jnp.int32, sums.shape, 1)
    rr, rn, nn, ww = (jnp.sum(jnp.where(lane == i, sums, 0.0), axis=1, keepdims=True) for i in range(4))
    alpha = rr / rn
    new = rr - 2.0 * alpha * rn + alpha * alpha * nn
    beta = new / rr
    grow = 1.0 + beta
    curve = grow * grow * rn - 2.0 * alpha * grow * nn + alpha * alpha * (ww + ridge * nn)
    step = new / curve
    left = alpha + step * grow
    right = -step * alpha
    out_ref[core[0]] = left * keep_ref[0] + right * keep_ref[1]
    out_ref[1 - core[0]] = left * got_ref[0] + right * got_ref[1]


def finish(core, ridge, sums, keep, got):
    return pl.pallas_call(
        lambda *refs: finish_kernel(ridge, *refs),
        grid_spec=pltpu.PrefetchScalarGridSpec(
            num_scalar_prefetch=1,
            grid=(1,),
            in_specs=[whole(sums.shape), whole(keep.shape), whole(got.shape)],
            out_specs=whole(keep.shape),
        ),
        out_shape=jax.ShapeDtypeStruct(keep.shape, f32),
        compiler_params=params(4),
        name="finish",
    )(core, sums, keep, got)


def local(history_keys, history_values, queries, positions, kept_index):
    count = kept_index.shape[1]
    own_rows = queries.shape[1]
    devices = lax.axis_size(("chip", "core"))
    everyone = lax.axis_size("head") * devices
    ridge = own_rows * devices / (count * count)
    index = lax.axis_index("core")
    core = index.astype(jnp.int32).reshape(1)
    swap = [(0, 1), (1, 0)]

    history_keys, history_values, queries, positions, kept_index = (
        pltpu.with_memory_space_constraint(x, pltpu.HBM)
        for x in (history_keys, history_values, queries, positions, kept_index)
    )

    mine, send, kept = pack(core, queries, positions, kept_index)
    other = lax.ppermute(send, "core", swap)
    target, q, pos, kept_keys, kept_values = attend(core, mine, other, kept, history_keys, history_values)
    expo, over, z = start(core, q, pos, kept, kept_keys, kept_values, target)

    def exchange(chunks):
        return lax.all_to_all(chunks, "chip", 0, 0, tiled=True)

    res, copies = fold(exchange(z))
    z = with_weights(
        normal_kernel, "normal", z.shape, exchange(copies), over, expo, scratch=[pltpu.VMEM((2 * HD, 2 * own_rows), bf16)]
    )
    copies, sums, keep, send = fold_image(core, ridge, exchange(z), res)
    copies, send = lax.optimization_barrier((exchange(copies), send))
    got = lax.ppermute(send, "core", swap)
    sums = with_weights(square_kernel, "square", (everyone, 1, LANES), copies, over, expo, sums)
    sums = lax.all_to_all(sums, ("head", "chip", "core"), 0, 0, tiled=True)
    return finish(core, ridge, sums, keep, got)


def solution(mesh):
    heads, probes = mesh.devices.shape
    split = Mesh(mesh.devices.reshape(heads, probes // 2, 2), ("head", "chip", "core"))
    probe = ("chip", "core")
    return jax.shard_map(
        local,
        mesh=split,
        in_specs=(
            P("head", None, None),
            P("head", None, None),
            P("head", probe, None),
            P("head", probe),
            P("head", None),
        ),
        out_specs=P("head", probe, None),
        check_vma=False,
    )
```

```python
import math

import jax
import jax.numpy as jnp
from jax import lax
from jax.experimental import pallas as pl
from jax.experimental.pallas import tpu as pltpu
from jax.sharding import Mesh
from jax.sharding import PartitionSpec as P

HD = 128
LANES = 128
BLOCK = 2048
ROWS = 256
PICK = 256
LIMIT = 2.0**40
SCALE = math.log2(math.e) / math.sqrt(HD)
MIB = 1024 * 1024
START = 32
WEIGHTS = 16
f32 = jnp.float32
bf16 = jnp.bfloat16
NT = (((1,), (1,)), ((), ()))
NN = (((1,), (0,)), ((), ()))


def dot(left, right, dims=NN):
    return lax.dot_general(left, right, dims, preferred_element_type=f32)


def halves(wide):
    high = wide.astype(bf16)
    return high, (wide - high.astype(f32)).astype(bf16)


def stacked(wide):
    return jnp.concatenate(halves(wide), axis=0)


def whole(shape):
    return pl.BlockSpec(shape, lambda *ids: (0,) * len(shape))


def params(mib):
    return pltpu.CompilerParams(vmem_limit_bytes=mib * MIB)


def columns_of(rows):
    return jnp.transpose(rows).astype(jnp.int32)


def stack_columns(cols, first, count):
    return jnp.concatenate([cols[:, i : i + 1] for i in range(first, first + count)], axis=0)


def row_of(ref, which, here):
    return jnp.where(which == 0, ref[0:1, here], ref[1:2, here])


def pack_kernel(core, q_ref, place_ref, kept_ref, mine_ref, send_ref, kept_out):
    own = q_ref.shape[1]
    lines = own // LANES
    for which, out_ref in ((core[0], mine_ref), (1 - core[0], send_ref)):
        out_ref[:own, :] = q_ref[which].astype(f32)
        for line in range(lines):
            here = pl.ds(line * LANES, LANES)
            out_ref[own + line : own + line + 1, :] = row_of(place_ref, which, here).astype(f32)
        out_ref[own + lines :, :] = jnp.zeros((8 - lines % 8, LANES), f32)
    kept_out[...] = kept_ref[...]


def pack(core, queries, positions, kept):
    own = queries.shape[1]
    lines = own // LANES
    out = (own + lines + 8 - lines % 8, HD)
    return pl.pallas_call(
        pack_kernel,
        grid_spec=pltpu.PrefetchScalarGridSpec(
            num_scalar_prefetch=1,
            grid=(1,),
            in_specs=[whole(queries.shape), whole(positions.shape), whole(kept.shape)],
            out_specs=[whole(out), whole(out), whole(kept.shape)],
        ),
        out_shape=[
            jax.ShapeDtypeStruct(out, f32),
            jax.ShapeDtypeStruct(out, f32),
            jax.ShapeDtypeStruct(kept.shape, jnp.int32),
        ],
        compiler_params=params(4),
        name="pack",
    )(core, queries, positions, kept)


def attend_kernel(core, mine_ref, other_ref, kept_ref, k_any, v_any, t_ref, q_ref, pos_ref, kk_ref, kv_ref, m_ref, acc_ref, v2_ref, k_buf, v_buf, sem):
    step = pl.program_id(0)
    steps = pl.num_programs(0)
    rows = q_ref.shape[0]
    own = rows // 2
    lines = own // LANES
    tiles = rows // ROWS
    slots = PICK // 8
    slot = lax.rem(step, 2)

    def copies(j, to):
        here = pl.ds(pl.multiple_of(j * BLOCK, BLOCK), BLOCK)
        return (
            pltpu.make_async_copy(k_any.at[core[0], here, :], k_buf.at[to], sem.at[0, to]),
            pltpu.make_async_copy(v_any.at[core[0], here, :], v_buf.at[to], sem.at[1, to]),
        )

    def fetch(j, to):
        for copy in copies(j, to):
            copy.start()

    def arrive(j, to):
        for copy in copies(j, to):
            copy.wait()

    @pl.when(step == 0)
    def _():
        fetch(0, 0)
        for part, ref in enumerate((mine_ref, other_ref)):
            q_ref[pl.ds(part * own, own), :] = ref[:own, :].astype(bf16)
            pos_ref[pl.ds(part * lines, lines), :] = ref[own : own + lines, :]
        m_ref[...] = jnp.full(m_ref.shape, -jnp.inf, f32)
        acc_ref[...] = jnp.zeros(acc_ref.shape, f32)
        v2_ref[:, HD:] = jnp.ones((BLOCK, HD), bf16)

    @pl.when(step + 1 < steps)
    def _():
        fetch(step + 1, 1 - slot)

    arrive(step, slot)

    def load(of):
        v2_ref[:, :HD] = v_buf[of]

    def pick():
        per = BLOCK // 8
        kept_row = kept_ref[pl.ds(core[0], 1), pl.ds(pl.multiple_of(step * per, per), per)] - step * BLOCK
        lane = lax.broadcasted_iota(jnp.int32, (slots, PICK), 1)
        for half in range(per // LANES):
            col = jnp.transpose(jnp.broadcast_to(kept_row[:, half * LANES : (half + 1) * LANES], (LANES, LANES)))[:, :1]
            for piece in range(LANES // slots):
                at = (half * LANES + piece * slots) * 8
                hot = jnp.where(lane == col[piece * slots : (piece + 1) * slots, :] - at, 1.0, 0.0).astype(bf16)
                both = jnp.concatenate([k_buf[slot, at : at + PICK, :], v_buf[slot, at : at + PICK, :]], axis=1)
                got = dot(hot, both).astype(bf16)
                here = pl.ds(half * LANES + piece * slots, slots)
                kk_ref[here, :] = got[:, :HD]
                kv_ref[here, :] = got[:, HD:]

    def scores_of(tile, of, base, masked):
        scores = dot(q_ref[pl.ds(tile * ROWS, ROWS), :], k_buf[of], NT) * SCALE
        if masked:
            cols = columns_of(pos_ref[...]) - base
            pos = stack_columns(cols, tile * ROWS // LANES, ROWS // LANES)
            lane = lax.broadcasted_iota(jnp.int32, scores.shape, 1)
            scores = jnp.where(lane <= pos, scores, -jnp.inf)
        return scores

    def tile_now(tile, of, base, masked, running):
        here = pl.ds(tile * ROWS, ROWS)
        scores = scores_of(tile, of, base, masked)
        if not running:
            expo = jnp.exp2(scores - m_ref[here, :1]).astype(bf16)
            acc_ref[here, :] += dot(expo, v2_ref[...])
            return
        old = m_ref[here, :]
        new = jnp.maximum(old, jnp.max(scores, axis=1, keepdims=True))
        m_ref[here, :] = new
        expo = jnp.exp2(scores - new[:, :1]).astype(bf16)
        fade = jnp.exp2(old - new)
        both = jnp.concatenate([fade, fade], axis=1)
        acc_ref[here, :] = acc_ref[here, :] * both + dot(expo, v2_ref[...])

    def go(masked, running):
        load(slot)
        for tile in range(tiles):
            tile_now(tile, slot, step * BLOCK, masked, running)
        pick()

    early = step < steps // 2
    follow = (step == 0) | ((core[0] == 0) & (step >= steps // 2))
    for masked in (False, True):
        for running in (False, True):

            @pl.when((early != masked) & (follow == running))
            def _(masked=masked, running=running):
                go(masked, running)

    @pl.when((step == steps - 1) & jnp.logical_not(jnp.max(jnp.max(acc_ref[:, HD : HD + 1], axis=0, keepdims=True)) <= LIMIT))
    def _():
        m_ref[...] = jnp.full(m_ref.shape, -jnp.inf, f32)
        acc_ref[...] = jnp.zeros(acc_ref.shape, f32)

        def block(j, carry):
            fetch(j, 0)
            arrive(j, 0)
            load(0)
            for tile in range(tiles):
                tile_now(tile, 0, j * BLOCK, True, True)
            return carry

        lax.fori_loop(0, steps, block, 0)

    @pl.when(step == steps - 1)
    def _():
        t_ref[...] = acc_ref[:, :HD] / acc_ref[:, HD:]


def attend(core, mine, other, kept, keys, values):
    rows = 2 * (mine.shape[0] // LANES * LANES)
    steps = keys.shape[1] // BLOCK
    count = kept.shape[1]
    per = BLOCK // 8
    return pl.pallas_call(
        attend_kernel,
        grid_spec=pltpu.PrefetchScalarGridSpec(
            num_scalar_prefetch=1,
            grid=(steps,),
            in_specs=[
                whole(mine.shape),
                whole(other.shape),
                whole(kept.shape),
                pl.BlockSpec(memory_space=pltpu.HBM),
                pl.BlockSpec(memory_space=pltpu.HBM),
            ],
            out_specs=[
                whole((rows, HD)),
                whole((rows, HD)),
                whole((rows // LANES, LANES)),
                pl.BlockSpec((per, HD), lambda j, c: (j, 0)),
                pl.BlockSpec((per, HD), lambda j, c: (j, 0)),
            ],
            scratch_shapes=[
                pltpu.VMEM((rows, LANES), f32),
                pltpu.VMEM((rows, 2 * HD), f32),
                pltpu.VMEM((BLOCK, 2 * HD), bf16),
                pltpu.VMEM((2, BLOCK, HD), bf16),
                pltpu.VMEM((2, BLOCK, HD), bf16),
                pltpu.SemaphoreType.DMA((2, 2)),
            ],
        ),
        out_shape=[
            jax.ShapeDtypeStruct((rows, HD), f32),
            jax.ShapeDtypeStruct((rows, HD), bf16),
            jax.ShapeDtypeStruct((rows // LANES, LANES), f32),
            jax.ShapeDtypeStruct((count, HD), bf16),
            jax.ShapeDtypeStruct((count, HD), bf16),
        ],
        compiler_params=params(40),
        name="attend",
    )(core, mine, other, kept, keys, values)


def put_chunks(z_ref, rows):
    for chunk in range(z_ref.shape[0]):
        z_ref[chunk] = rows[:, chunk * LANES : (chunk + 1) * LANES]


def pulled(two, expo):
    back = dot(two, expo)
    return back[:HD] + back[HD:]


def start_kernel(core, q_ref, pos_ref, kept_ref, kk_ref, kv_ref, t_ref, e_ref, over_ref, z_ref, low_ref, two_ref):
    kept = kept_ref[pl.ds(core[0], 1), :]
    cols = columns_of(pos_ref[...])
    values = jnp.concatenate([kv_ref[...], kv_ref[...]], axis=0)
    for tile in range(e_ref.shape[0] // ROWS):
        here = pl.ds(tile * ROWS, ROWS)
        scores = dot(q_ref[here, :], kk_ref[...], NT) * SCALE
        pos = stack_columns(cols, tile * ROWS // LANES, ROWS // LANES)
        scores = jnp.where(kept <= pos, scores, -jnp.inf)
        expo = jnp.exp2(scores - jnp.max(scores, axis=1, keepdims=True))
        over = 1.0 / jnp.sum(expo, axis=1, keepdims=True)
        high, low = halves(expo)
        e_ref[here, :] = high
        low_ref[here, :] = low
        gap = t_ref[here, :] - dot(jnp.concatenate([high, low], axis=1), values) * over
        over_ref[:, here] = jnp.transpose(jnp.broadcast_to(over, (ROWS, LANES)))[:8, :]
        two_ref[:, here] = stacked(jnp.transpose(gap * over))
    put_chunks(z_ref, pulled(two_ref[...], e_ref[...]) + dot(two_ref[:HD, :], low_ref[...]))


def start(core, q, pos, kept, kept_keys, kept_values, target):
    rows = q.shape[0]
    count = kept_keys.shape[0]
    inputs = (q, pos, kept, kept_keys, kept_values, target)
    return pl.pallas_call(
        start_kernel,
        grid_spec=pltpu.PrefetchScalarGridSpec(
            num_scalar_prefetch=1,
            grid=(1,),
            in_specs=[whole(x.shape) for x in inputs],
            out_specs=[
                whole((rows, count)),
                whole((8, rows)),
                whole((count // LANES, HD, LANES)),
            ],
            scratch_shapes=[
                pltpu.VMEM((rows, count), bf16),
                pltpu.VMEM((2 * HD, rows), bf16),
            ],
        ),
        out_shape=[
            jax.ShapeDtypeStruct((rows, count), bf16),
            jax.ShapeDtypeStruct((8, rows), f32),
            jax.ShapeDtypeStruct((count // LANES, HD, LANES), f32),
        ],
        compiler_params=params(START),
        name="start",
    )(core, *inputs)


def load_vector(vec_ref, two_ref):
    for chunk in range(vec_ref.shape[0]):
        two_ref[:, chunk * LANES : (chunk + 1) * LANES] = stacked(vec_ref[chunk])


def tiles_of(e_ref):
    return [pl.ds(tile * ROWS, ROWS) for tile in range(e_ref.shape[0] // ROWS)]


def pushed(vec_ref, here, e_ref):
    two = dot(vec_ref[...], e_ref[here, :], NT)
    return two[:HD] + two[HD:]


def normal_kernel(vec_ref, over_ref, e_ref, z_ref, two_ref, image_ref):
    load_vector(vec_ref, two_ref)
    for here in tiles_of(e_ref):
        over = over_ref[:1, here]
        image_ref[:, here] = stacked(pushed(two_ref, here, e_ref) * (over * over))
    put_chunks(z_ref, pulled(image_ref[...], e_ref[...]))


def square_kernel(vec_ref, over_ref, e_ref, sums_ref, s_ref, two_ref):
    load_vector(vec_ref, two_ref)
    total = jnp.zeros((1, ROWS), f32)
    for here in tiles_of(e_ref):
        image = pushed(two_ref, here, e_ref) * over_ref[:1, here]
        total += jnp.sum(image * image, axis=0, keepdims=True)
    last = sum(total[:, i * LANES : (i + 1) * LANES] for i in range(ROWS // LANES))
    row = lax.broadcasted_iota(jnp.int32, sums_ref.shape, 0)
    lane = lax.broadcasted_iota(jnp.int32, sums_ref.shape, 1)
    sums = jnp.sum(jnp.where(row == 3, last, sums_ref[...]), axis=1, keepdims=True)
    line = jnp.sum(jnp.where(row == lane, sums, 0.0), axis=0, keepdims=True)
    s_ref[...] = jnp.broadcast_to(line[None], s_ref.shape)


def with_weights(kernel, name, out, vec, over, expo, *more, scratch=()):
    rows, count = expo.shape
    return pl.pallas_call(
        kernel,
        in_specs=[whole(vec.shape), whole(over.shape), whole(expo.shape)] + [whole(a.shape) for a in more],
        out_specs=whole(out),
        out_shape=jax.ShapeDtypeStruct(out, f32),
        scratch_shapes=[
            pltpu.VMEM((2 * HD, count), bf16),
            *scratch,
        ],
        compiler_params=params(WEIGHTS),
        name=name,
    )(vec, over, expo, *more)


def fold_kernel(parts_ref, chunk_ref, copies_ref):
    total = jnp.sum(parts_ref[...], axis=0)
    chunk_ref[...] = total
    copies_ref[...] = jnp.broadcast_to(total[None], copies_ref.shape)


def fold(parts):
    return pl.pallas_call(
        fold_kernel,
        in_specs=[whole(parts.shape)],
        out_specs=[whole(parts.shape[1:]), whole(parts.shape)],
        out_shape=[jax.ShapeDtypeStruct(parts.shape[1:], f32), jax.ShapeDtypeStruct(parts.shape, f32)],
        compiler_params=params(8),
        name="fold",
    )(parts)


def fold_image_kernel(ridge, core, parts_ref, res_ref, copies_ref, sums_ref, keep_ref, send_ref, turn_ref):
    res = res_ref[...]
    total = jnp.sum(parts_ref[...], axis=0) + ridge * res
    copies_ref[...] = jnp.broadcast_to(total[None], copies_ref.shape)
    sums_ref[...] = jnp.zeros(sums_ref.shape, f32)
    sums_ref[0:1, :] = jnp.sum(res * res, axis=0, keepdims=True)
    sums_ref[1:2, :] = jnp.sum(res * total, axis=0, keepdims=True)
    sums_ref[2:3, :] = jnp.sum(total * total, axis=0, keepdims=True)
    half = keep_ref.shape[1]
    for i, chunk in enumerate((res, total)):
        turn_ref[...] = jnp.transpose(chunk)
        keep_ref[i] = turn_ref[pl.ds(pl.multiple_of(core[0] * half, half), half), :]
        send_ref[i] = turn_ref[pl.ds(pl.multiple_of((1 - core[0]) * half, half), half), :]


def fold_image(core, ridge, parts, res):
    half = (2, parts.shape[2] // 2, HD)
    return pl.pallas_call(
        lambda *refs: fold_image_kernel(ridge, *refs),
        grid_spec=pltpu.PrefetchScalarGridSpec(
            num_scalar_prefetch=1,
            grid=(1,),
            in_specs=[whole(parts.shape), whole(res.shape)],
            out_specs=[whole(parts.shape), whole((8, LANES)), whole(half), whole(half)],
            scratch_shapes=[pltpu.VMEM(res.shape, f32)],
        ),
        out_shape=[
            jax.ShapeDtypeStruct(parts.shape, f32),
            jax.ShapeDtypeStruct((8, LANES), f32),
            jax.ShapeDtypeStruct(half, f32),
            jax.ShapeDtypeStruct(half, f32),
        ],
        compiler_params=params(8),
        name="fold_image",
    )(core, parts, res)


def finish_kernel(ridge, core, sums_ref, keep_ref, got_ref, out_ref):
    sums = jnp.sum(sums_ref[...], axis=0)
    lane = lax.broadcasted_iota(jnp.int32, sums.shape, 1)
    rr, rn, nn, ww = (jnp.sum(jnp.where(lane == i, sums, 0.0), axis=1, keepdims=True) for i in range(4))
    alpha = rr / rn
    new = rr - 2.0 * alpha * rn + alpha * alpha * nn
    beta = new / rr
    grow = 1.0 + beta
    curve = grow * grow * rn - 2.0 * alpha * grow * nn + alpha * alpha * (ww + ridge * nn)
    step = new / curve
    left = alpha + step * grow
    right = -step * alpha
    out_ref[core[0]] = left * keep_ref[0] + right * keep_ref[1]
    out_ref[1 - core[0]] = left * got_ref[0] + right * got_ref[1]


def finish(core, ridge, sums, keep, got):
    return pl.pallas_call(
        lambda *refs: finish_kernel(ridge, *refs),
        grid_spec=pltpu.PrefetchScalarGridSpec(
            num_scalar_prefetch=1,
            grid=(1,),
            in_specs=[whole(sums.shape), whole(keep.shape), whole(got.shape)],
            out_specs=whole(keep.shape),
        ),
        out_shape=jax.ShapeDtypeStruct(keep.shape, f32),
        compiler_params=params(4),
        name="finish",
    )(core, sums, keep, got)


def local(history_keys, history_values, queries, positions, kept_index):
    count = kept_index.shape[1]
    own_rows = queries.shape[1]
    devices = lax.axis_size(("chip", "core"))
    everyone = lax.axis_size("head") * devices
    ridge = own_rows * devices / (count * count)
    index = lax.axis_index("core")
    core = index.astype(jnp.int32).reshape(1)
    swap = [(0, 1), (1, 0)]

    history_keys, history_values, queries, positions, kept_index = (
        pltpu.with_memory_space_constraint(x, pltpu.HBM)
        for x in (history_keys, history_values, queries, positions, kept_index)
    )

    mine, send, kept = pack(core, queries, positions, kept_index)
    other = lax.ppermute(send, "core", swap)
    target, q, pos, kept_keys, kept_values = attend(core, mine, other, kept, history_keys, history_values)
    expo, over, z = start(core, q, pos, kept, kept_keys, kept_values, target)

    def exchange(chunks):
        return lax.all_to_all(chunks, "chip", 0, 0, tiled=True)

    res, copies = fold(exchange(z))
    z = with_weights(
        normal_kernel, "normal", z.shape, exchange(copies), over, expo, scratch=[pltpu.VMEM((2 * HD, 2 * own_rows), bf16)]
    )
    copies, sums, keep, send = fold_image(core, ridge, exchange(z), res)
    copies, send = lax.optimization_barrier((exchange(copies), send))
    got = lax.ppermute(send, "core", swap)
    sums = with_weights(square_kernel, "square", (everyone, 1, LANES), copies, over, expo, sums)
    sums = lax.all_to_all(sums, ("head", "chip", "core"), 0, 0, tiled=True)
    return finish(core, ridge, sums, keep, got)


def solution(mesh):
    heads, probes = mesh.devices.shape
    split = Mesh(mesh.devices.reshape(heads, probes // 2, 2), ("head", "chip", "core"))
    probe = ("chip", "core")
    return jax.shard_map(
        local,
        mesh=split,
        in_specs=(
            P("head", None, None),
            P("head", None, None),
            P("head", probe, None),
            P("head", probe),
            P("head", None),
        ),
        out_specs=P("head", probe, None),
        check_vma=False,
    )
```

```python
import math

import jax
import jax.numpy as jnp
from jax import lax
from jax.experimental import pallas as pl
from jax.experimental.pallas import tpu as pltpu
from jax.sharding import Mesh
from jax.sharding import PartitionSpec as P

HD = 128
LANES = 128
BLOCK = 2048
ROWS = 256
PICK = 256
LIMIT = 2.0**40
SCALE = math.log2(math.e) / math.sqrt(HD)
MIB = 1024 * 1024
START = 32
WEIGHTS = 16
f32 = jnp.float32
bf16 = jnp.bfloat16
NT = (((1,), (1,)), ((), ()))
NN = (((1,), (0,)), ((), ()))


def dot(left, right, dims=NN):
    return lax.dot_general(left, right, dims, preferred_element_type=f32)


def halves(wide):
    high = wide.astype(bf16)
    return high, (wide - high.astype(f32)).astype(bf16)


def stacked(wide):
    return jnp.concatenate(halves(wide), axis=0)


def whole(shape):
    return pl.BlockSpec(shape, lambda *ids: (0,) * len(shape))


def params(mib):
    return pltpu.CompilerParams(vmem_limit_bytes=mib * MIB)


def columns_of(rows):
    return jnp.transpose(rows).astype(jnp.int32)


def stack_columns(cols, first, count):
    return jnp.concatenate([cols[:, i : i + 1] for i in range(first, first + count)], axis=0)


def row_of(ref, which, here):
    return jnp.where(which == 0, ref[0:1, here], ref[1:2, here])


def pack_kernel(core, q_ref, place_ref, kept_ref, mine_ref, send_ref, kept_out):
    own = q_ref.shape[1]
    lines = own // LANES
    for which, out_ref in ((core[0], mine_ref), (1 - core[0], send_ref)):
        out_ref[:own, :] = q_ref[which].astype(f32)
        for line in range(lines):
            here = pl.ds(line * LANES, LANES)
            out_ref[own + line : own + line + 1, :] = row_of(place_ref, which, here).astype(f32)
        out_ref[own + lines :, :] = jnp.zeros((8 - lines % 8, LANES), f32)
    kept_out[...] = kept_ref[...]


def pack(core, queries, positions, kept):
    own = queries.shape[1]
    lines = own // LANES
    out = (own + lines + 8 - lines % 8, HD)
    return pl.pallas_call(
        pack_kernel,
        grid_spec=pltpu.PrefetchScalarGridSpec(
            num_scalar_prefetch=1,
            grid=(1,),
            in_specs=[whole(queries.shape), whole(positions.shape), whole(kept.shape)],
            out_specs=[whole(out), whole(out), whole(kept.shape)],
        ),
        out_shape=[
            jax.ShapeDtypeStruct(out, f32),
            jax.ShapeDtypeStruct(out, f32),
            jax.ShapeDtypeStruct(kept.shape, jnp.int32),
        ],
        compiler_params=params(4),
        name="pack",
    )(core, queries, positions, kept)


def attend_kernel(core, mine_ref, other_ref, kept_ref, k_any, v_any, t_ref, q_ref, pos_ref, kk_ref, kv_ref, m_ref, acc_ref, v2_ref, k_buf, v_buf, sem):
    step = pl.program_id(0)
    steps = pl.num_programs(0)
    rows = q_ref.shape[0]
    own = rows // 2
    lines = own // LANES
    tiles = rows // ROWS
    slots = PICK // 8
    slot = lax.rem(step, 2)

    def copies(j, to):
        here = pl.ds(pl.multiple_of(j * BLOCK, BLOCK), BLOCK)
        return (
            pltpu.make_async_copy(k_any.at[core[0], here, :], k_buf.at[to], sem.at[0, to]),
            pltpu.make_async_copy(v_any.at[core[0], here, :], v_buf.at[to], sem.at[1, to]),
        )

    def fetch(j, to):
        for copy in copies(j, to):
            copy.start()

    def arrive(j, to):
        for copy in copies(j, to):
            copy.wait()

    @pl.when(step == 0)
    def _():
        fetch(0, 0)
        for part, ref in enumerate((mine_ref, other_ref)):
            q_ref[pl.ds(part * own, own), :] = ref[:own, :].astype(bf16)
            pos_ref[pl.ds(part * lines, lines), :] = ref[own : own + lines, :]
        m_ref[...] = jnp.full(m_ref.shape, -jnp.inf, f32)
        acc_ref[...] = jnp.zeros(acc_ref.shape, f32)
        v2_ref[:, HD:] = jnp.ones((BLOCK, HD), bf16)

    @pl.when(step + 1 < steps)
    def _():
        fetch(step + 1, 1 - slot)

    arrive(step, slot)

    def load(of):
        v2_ref[:, :HD] = v_buf[of]

    def pick():
        per = BLOCK // 8
        kept_row = kept_ref[pl.ds(core[0], 1), pl.ds(pl.multiple_of(step * per, per), per)] - step * BLOCK
        lane = lax.broadcasted_iota(jnp.int32, (slots, PICK), 1)
        for half in range(per // LANES):
            col = jnp.transpose(jnp.broadcast_to(kept_row[:, half * LANES : (half + 1) * LANES], (LANES, LANES)))[:, :1]
            for piece in range(LANES // slots):
                at = (half * LANES + piece * slots) * 8
                hot = jnp.where(lane == col[piece * slots : (piece + 1) * slots, :] - at, 1.0, 0.0).astype(bf16)
                both = jnp.concatenate([k_buf[slot, at : at + PICK, :], v_buf[slot, at : at + PICK, :]], axis=1)
                got = dot(hot, both).astype(bf16)
                here = pl.ds(half * LANES + piece * slots, slots)
                kk_ref[here, :] = got[:, :HD]
                kv_ref[here, :] = got[:, HD:]

    def scores_of(tile, of, base, masked):
        scores = dot(q_ref[pl.ds(tile * ROWS, ROWS), :], k_buf[of], NT) * SCALE
        if masked:
            cols = columns_of(pos_ref[...]) - base
            pos = stack_columns(cols, tile * ROWS // LANES, ROWS // LANES)
            lane = lax.broadcasted_iota(jnp.int32, scores.shape, 1)
            scores = jnp.where(lane <= pos, scores, -jnp.inf)
        return scores

    def tile_now(tile, of, base, masked, running):
        here = pl.ds(tile * ROWS, ROWS)
        scores = scores_of(tile, of, base, masked)
        if not running:
            expo = jnp.exp2(scores - m_ref[here, :1]).astype(bf16)
            acc_ref[here, :] += dot(expo, v2_ref[...])
            return
        old = m_ref[here, :]
        new = jnp.maximum(old, jnp.max(scores, axis=1, keepdims=True))
        m_ref[here, :] = new
        expo = jnp.exp2(scores - new[:, :1]).astype(bf16)
        fade = jnp.exp2(old - new)
        both = jnp.concatenate([fade, fade], axis=1)
        acc_ref[here, :] = acc_ref[here, :] * both + dot(expo, v2_ref[...])

    def go(masked, running):
        load(slot)
        for tile in range(tiles):
            tile_now(tile, slot, step * BLOCK, masked, running)
        pick()

    early = step < steps // 2
    follow = (step == 0) | ((core[0] == 0) & (step >= steps // 2))
    for masked in (False, True):
        for running in (False, True):

            @pl.when((early != masked) & (follow == running))
            def _(masked=masked, running=running):
                go(masked, running)

    @pl.when(step == steps - 1)
    def _():
        largest = jnp.max(jnp.max(acc_ref[:, HD : HD + 1], axis=0, keepdims=True))

        @pl.when(jnp.logical_not(largest <= LIMIT))
        def _():
            m_ref[...] = jnp.full(m_ref.shape, -jnp.inf, f32)
            acc_ref[...] = jnp.zeros(acc_ref.shape, f32)

            def block(j, carry):
                fetch(j, 0)
                arrive(j, 0)
                load(0)
                for tile in range(tiles):
                    tile_now(tile, 0, j * BLOCK, True, True)
                return carry

            lax.fori_loop(0, steps, block, 0)

    @pl.when(step == steps - 1)
    def _():
        t_ref[...] = acc_ref[:, :HD] / acc_ref[:, HD:]


def attend(core, mine, other, kept, keys, values):
    rows = 2 * (mine.shape[0] // LANES * LANES)
    steps = keys.shape[1] // BLOCK
    count = kept.shape[1]
    per = BLOCK // 8
    return pl.pallas_call(
        attend_kernel,
        grid_spec=pltpu.PrefetchScalarGridSpec(
            num_scalar_prefetch=1,
            grid=(steps,),
            in_specs=[
                whole(mine.shape),
                whole(other.shape),
                whole(kept.shape),
                pl.BlockSpec(memory_space=pltpu.HBM),
                pl.BlockSpec(memory_space=pltpu.HBM),
            ],
            out_specs=[
                whole((rows, HD)),
                whole((rows, HD)),
                whole((rows // LANES, LANES)),
                pl.BlockSpec((per, HD), lambda j, c: (j, 0)),
                pl.BlockSpec((per, HD), lambda j, c: (j, 0)),
            ],
            scratch_shapes=[
                pltpu.VMEM((rows, LANES), f32),
                pltpu.VMEM((rows, 2 * HD), f32),
                pltpu.VMEM((BLOCK, 2 * HD), bf16),
                pltpu.VMEM((2, BLOCK, HD), bf16),
                pltpu.VMEM((2, BLOCK, HD), bf16),
                pltpu.SemaphoreType.DMA((2, 2)),
            ],
        ),
        out_shape=[
            jax.ShapeDtypeStruct((rows, HD), f32),
            jax.ShapeDtypeStruct((rows, HD), bf16),
            jax.ShapeDtypeStruct((rows // LANES, LANES), f32),
            jax.ShapeDtypeStruct((count, HD), bf16),
            jax.ShapeDtypeStruct((count, HD), bf16),
        ],
        compiler_params=params(40),
        name="attend",
    )(core, mine, other, kept, keys, values)


def put_chunks(z_ref, rows):
    for chunk in range(z_ref.shape[0]):
        z_ref[chunk] = rows[:, chunk * LANES : (chunk + 1) * LANES]


def pulled(two, expo):
    back = dot(two, expo)
    return back[:HD] + back[HD:]


def start_kernel(core, q_ref, pos_ref, kept_ref, kk_ref, kv_ref, t_ref, e_ref, over_ref, z_ref, low_ref, two_ref):
    kept = kept_ref[pl.ds(core[0], 1), :]
    cols = columns_of(pos_ref[...])
    values = jnp.concatenate([kv_ref[...], kv_ref[...]], axis=0)
    for tile in range(e_ref.shape[0] // ROWS):
        here = pl.ds(tile * ROWS, ROWS)
        scores = dot(q_ref[here, :], kk_ref[...], NT) * SCALE
        pos = stack_columns(cols, tile * ROWS // LANES, ROWS // LANES)
        scores = jnp.where(kept <= pos, scores, -jnp.inf)
        expo = jnp.exp2(scores - jnp.max(scores, axis=1, keepdims=True))
        over = 1.0 / jnp.sum(expo, axis=1, keepdims=True)
        high, low = halves(expo)
        e_ref[here, :] = high
        low_ref[here, :] = low
        gap = t_ref[here, :] - dot(jnp.concatenate([high, low], axis=1), values) * over
        over_ref[:, here] = jnp.transpose(jnp.broadcast_to(over, (ROWS, LANES)))[:8, :]
        two_ref[:, here] = stacked(jnp.transpose(gap * over))
    put_chunks(z_ref, pulled(two_ref[...], e_ref[...]) + dot(two_ref[:HD, :], low_ref[...]))


def start(core, q, pos, kept, kept_keys, kept_values, target):
    rows = q.shape[0]
    count = kept_keys.shape[0]
    inputs = (q, pos, kept, kept_keys, kept_values, target)
    return pl.pallas_call(
        start_kernel,
        grid_spec=pltpu.PrefetchScalarGridSpec(
            num_scalar_prefetch=1,
            grid=(1,),
            in_specs=[whole(x.shape) for x in inputs],
            out_specs=[
                whole((rows, count)),
                whole((8, rows)),
                whole((count // LANES, HD, LANES)),
            ],
            scratch_shapes=[
                pltpu.VMEM((rows, count), bf16),
                pltpu.VMEM((2 * HD, rows), bf16),
            ],
        ),
        out_shape=[
            jax.ShapeDtypeStruct((rows, count), bf16),
            jax.ShapeDtypeStruct((8, rows), f32),
            jax.ShapeDtypeStruct((count // LANES, HD, LANES), f32),
        ],
        compiler_params=params(START),
        name="start",
    )(core, *inputs)


def load_vector(vec_ref, two_ref):
    for chunk in range(vec_ref.shape[0]):
        two_ref[:, chunk * LANES : (chunk + 1) * LANES] = stacked(vec_ref[chunk])


def tiles_of(e_ref):
    return [pl.ds(tile * ROWS, ROWS) for tile in range(e_ref.shape[0] // ROWS)]


def pushed(vec_ref, here, e_ref):
    two = dot(vec_ref[...], e_ref[here, :], NT)
    return two[:HD] + two[HD:]


def normal_kernel(vec_ref, over_ref, e_ref, z_ref, two_ref, image_ref):
    load_vector(vec_ref, two_ref)
    for here in tiles_of(e_ref):
        over = over_ref[:1, here]
        image_ref[:, here] = stacked(pushed(two_ref, here, e_ref) * (over * over))
    put_chunks(z_ref, pulled(image_ref[...], e_ref[...]))


def square_kernel(vec_ref, over_ref, e_ref, sums_ref, s_ref, two_ref):
    load_vector(vec_ref, two_ref)
    total = jnp.zeros((1, ROWS), f32)
    for here in tiles_of(e_ref):
        image = pushed(two_ref, here, e_ref) * over_ref[:1, here]
        total += jnp.sum(image * image, axis=0, keepdims=True)
    last = sum(total[:, i * LANES : (i + 1) * LANES] for i in range(ROWS // LANES))
    row = lax.broadcasted_iota(jnp.int32, sums_ref.shape, 0)
    lane = lax.broadcasted_iota(jnp.int32, sums_ref.shape, 1)
    sums = jnp.sum(jnp.where(row == 3, last, sums_ref[...]), axis=1, keepdims=True)
    line = jnp.sum(jnp.where(row == lane, sums, 0.0), axis=0, keepdims=True)
    s_ref[...] = jnp.broadcast_to(line[None], s_ref.shape)


def with_weights(kernel, name, out, vec, over, expo, *more, scratch=()):
    rows, count = expo.shape
    return pl.pallas_call(
        kernel,
        in_specs=[whole(vec.shape), whole(over.shape), whole(expo.shape)] + [whole(a.shape) for a in more],
        out_specs=whole(out),
        out_shape=jax.ShapeDtypeStruct(out, f32),
        scratch_shapes=[
            pltpu.VMEM((2 * HD, count), bf16),
            *scratch,
        ],
        compiler_params=params(WEIGHTS),
        name=name,
    )(vec, over, expo, *more)


def fold_kernel(parts_ref, chunk_ref, copies_ref):
    total = jnp.sum(parts_ref[...], axis=0)
    chunk_ref[...] = total
    copies_ref[...] = jnp.broadcast_to(total[None], copies_ref.shape)


def fold(parts):
    return pl.pallas_call(
        fold_kernel,
        in_specs=[whole(parts.shape)],
        out_specs=[whole(parts.shape[1:]), whole(parts.shape)],
        out_shape=[jax.ShapeDtypeStruct(parts.shape[1:], f32), jax.ShapeDtypeStruct(parts.shape, f32)],
        compiler_params=params(8),
        name="fold",
    )(parts)


def fold_image_kernel(ridge, core, parts_ref, res_ref, copies_ref, sums_ref, keep_ref, send_ref, turn_ref):
    res = res_ref[...]
    total = jnp.sum(parts_ref[...], axis=0) + ridge * res
    copies_ref[...] = jnp.broadcast_to(total[None], copies_ref.shape)
    sums_ref[...] = jnp.zeros(sums_ref.shape, f32)
    sums_ref[0:1, :] = jnp.sum(res * res, axis=0, keepdims=True)
    sums_ref[1:2, :] = jnp.sum(res * total, axis=0, keepdims=True)
    sums_ref[2:3, :] = jnp.sum(total * total, axis=0, keepdims=True)
    half = keep_ref.shape[1]
    for i, chunk in enumerate((res, total)):
        turn_ref[...] = jnp.transpose(chunk)
        keep_ref[i] = turn_ref[pl.ds(pl.multiple_of(core[0] * half, half), half), :]
        send_ref[i] = turn_ref[pl.ds(pl.multiple_of((1 - core[0]) * half, half), half), :]


def fold_image(core, ridge, parts, res):
    half = (2, parts.shape[2] // 2, HD)
    return pl.pallas_call(
        lambda *refs: fold_image_kernel(ridge, *refs),
        grid_spec=pltpu.PrefetchScalarGridSpec(
            num_scalar_prefetch=1,
            grid=(1,),
            in_specs=[whole(parts.shape), whole(res.shape)],
            out_specs=[whole(parts.shape), whole((8, LANES)), whole(half), whole(half)],
            scratch_shapes=[pltpu.VMEM(res.shape, f32)],
        ),
        out_shape=[
            jax.ShapeDtypeStruct(parts.shape, f32),
            jax.ShapeDtypeStruct((8, LANES), f32),
            jax.ShapeDtypeStruct(half, f32),
            jax.ShapeDtypeStruct(half, f32),
        ],
        compiler_params=params(8),
        name="fold_image",
    )(core, parts, res)


def finish_kernel(ridge, core, sums_ref, keep_ref, got_ref, out_ref):
    sums = jnp.sum(sums_ref[...], axis=0)
    lane = lax.broadcasted_iota(jnp.int32, sums.shape, 1)
    rr, rn, nn, ww = (jnp.sum(jnp.where(lane == i, sums, 0.0), axis=1, keepdims=True) for i in range(4))
    alpha = rr / rn
    new = rr - 2.0 * alpha * rn + alpha * alpha * nn
    beta = new / rr
    grow = 1.0 + beta
    curve = grow * grow * rn - 2.0 * alpha * grow * nn + alpha * alpha * (ww + ridge * nn)
    step = new / curve
    left = alpha + step * grow
    right = -step * alpha
    out_ref[core[0]] = left * keep_ref[0] + right * keep_ref[1]
    out_ref[1 - core[0]] = left * got_ref[0] + right * got_ref[1]


def finish(core, ridge, sums, keep, got):
    return pl.pallas_call(
        lambda *refs: finish_kernel(ridge, *refs),
        grid_spec=pltpu.PrefetchScalarGridSpec(
            num_scalar_prefetch=1,
            grid=(1,),
            in_specs=[whole(sums.shape), whole(keep.shape), whole(got.shape)],
            out_specs=whole(keep.shape),
        ),
        out_shape=jax.ShapeDtypeStruct(keep.shape, f32),
        compiler_params=params(4),
        name="finish",
    )(core, sums, keep, got)


def local(history_keys, history_values, queries, positions, kept_index):
    count = kept_index.shape[1]
    own_rows = queries.shape[1]
    devices = lax.axis_size(("chip", "core"))
    everyone = lax.axis_size("head") * devices
    ridge = own_rows * devices / (count * count)
    index = lax.axis_index("core")
    core = index.astype(jnp.int32).reshape(1)
    swap = [(0, 1), (1, 0)]

    history_keys, history_values, queries, positions, kept_index = (
        pltpu.with_memory_space_constraint(x, pltpu.HBM)
        for x in (history_keys, history_values, queries, positions, kept_index)
    )

    mine, send, kept = pack(core, queries, positions, kept_index)
    other = lax.ppermute(send, "core", swap)
    target, q, pos, kept_keys, kept_values = attend(core, mine, other, kept, history_keys, history_values)
    expo, over, z = start(core, q, pos, kept, kept_keys, kept_values, target)

    def exchange(chunks):
        return lax.all_to_all(chunks, "chip", 0, 0, tiled=True)

    res, copies = fold(exchange(z))
    z = with_weights(
        normal_kernel, "normal", z.shape, exchange(copies), over, expo, scratch=[pltpu.VMEM((2 * HD, 2 * own_rows), bf16)]
    )
    copies, sums, keep, send = fold_image(core, ridge, exchange(z), res)
    copies, send = lax.optimization_barrier((exchange(copies), send))
    got = lax.ppermute(send, "core", swap)
    sums = with_weights(square_kernel, "square", (everyone, 1, LANES), copies, over, expo, sums)
    sums = lax.all_to_all(sums, ("head", "chip", "core"), 0, 0, tiled=True)
    return finish(core, ridge, sums, keep, got)


def solution(mesh):
    heads, probes = mesh.devices.shape
    split = Mesh(mesh.devices.reshape(heads, probes // 2, 2), ("head", "chip", "core"))
    probe = ("chip", "core")
    return jax.shard_map(
        local,
        mesh=split,
        in_specs=(
            P("head", None, None),
            P("head", None, None),
            P("head", probe, None),
            P("head", probe),
            P("head", None),
        ),
        out_specs=P("head", probe, None),
        check_vma=False,
    )
```
